32 devices in a mesh: gx: 4 (over y, core), gy: 8 (over z, x).
Axes of the slice: x: 2, y: 2, z: 4, core: 2. Of those that a mesh axis runs over, the one named last changes fastest.
Arguments:
- volume_sens: float32 [3, 128, 256, 128], P(None, 'gx', 'gy'), may hold values from -6 to 6
- stiffness: float32 [128, 256, 128], P('gx', 'gy'), may hold values from 0.25 to 4
- patch_of_row: int32 [32, 1024, 1], P(('gx', 'gy')), may hold values from 0 to 31; in each aligned block of 1024 rows (0 to 1023, 1024 to 2047, ..., all dimensions but the last counted through in order) at most 128 rows name the same one
- knot_spans: int32 [32, 1024, 2], P(('gx', 'gy')), may hold values from 0 to 60
- span_params: float32 [32, 1024, 2], P(('gx', 'gy')), may hold values from 0 to 1
Outputs:
- adjoint_field: float32 [3, 128, 256, 128], P(None, 'gx', 'gy')
- control_grad: float32 [32, 3, 64, 64], P(('gx', 'gy'))
The draws below stay inside these ranges and needn't reach their ends.
Inputs may be any that keep to these rules, and one draw needn't show every extreme that they name: `patch_of_row`: the surface nodes of one device name any one patch at most 128 times; in every draw some device names some patch exactly 128 times.
All inputs are finite; a program needn't handle non-finite values.
Results may differ from the reference program's by a relative error of at most 0.000092.
Values sent between devices are 32-bit elements; how exact they have to be, the bound alone decides.
A program may use at most 192 MiB of HBM per device.

```python
import math
import jax
import jax.numpy as jnp
import numpy as np

CX = 32
CY = 32
SWEEPS = 3
NC = 64
RS = 1024
CAP = 128
NX = 128
NY = 256
NZ = 128
PATCHES = 32
N_GX = 4
N_GY = 8
DEVICES = 32


def draw_stiffness(key, part):
    key_soft, key_stiff, key_linex, key_liney = jax.random.split(key, 4)
    shape = (NX, NY, NZ)
    soft = jnp.exp(jax.random.uniform(key_soft, shape, jnp.float32, math.log(0.25), math.log(0.8)))
    stiff = jnp.exp(jax.random.uniform(key_stiff, shape, jnp.float32, math.log(2.0), math.log(4.0)))
    share = 0.2
    along_x = jax.random.bernoulli(key_linex, share, (1, NY, NZ))
    along_y = jax.random.bernoulli(key_liney, share, (NX, 1, NZ))
    channel = jnp.logical_or(along_x, along_y)
    return jnp.clip(jnp.where(channel, stiff, soft), 0.25, 4.0).astype(jnp.float32)


def touch_ends(result, key, low, top_value):
    longest = result.shape.index(max(result.shape))
    spots = []
    for shift in (0, 1):
        where = [jax.random.randint(jax.random.fold_in(key, axis), (), 0, length) for axis, length in enumerate(result.shape)]
        where[longest] = (where[longest] + shift) % result.shape[longest]
        spots.append(tuple(where))
    return result.at[spots[0]].set(low).at[spots[1]].set(top_value)


def level_of(stream_key, shape, cuts, smallest, top_value):
    def one(dim, blocks):
        steps = jax.random.uniform(jax.random.fold_in(jax.random.fold_in(stream_key, 6), dim), (blocks,), jnp.float32, smallest / len(cuts), top_value / len(cuts))
        return jnp.repeat(jnp.exp(steps), shape[dim] // blocks).reshape((-1,) + (1,) * (len(shape) - dim - 1))

    gain = one(*cuts[0])
    for cut in cuts[1:]:
        gain = gain * one(*cut)
    return gain


def routed_block(stream_key, own, number, rows, number_of, top, reach, slope):
    sequence = jax.random.permutation(stream_key, number_of)
    packed, common = portions_of(number_of, rows * top, reach, slope, True), portions_of(number_of, rows * top, reach, slope, False)
    places = jnp.arange(number_of)

    def named(sizes, turn):
        used = int((sizes > 0).sum())
        fixed = max(1, used // 4)
        shifted = fixed + (places - fixed + turn * (used - fixed)) % max(1, number_of - fixed)
        return jnp.zeros((number_of,), jnp.int32).at[sequence[jnp.where(places < fixed, places, shifted)]].set(jnp.asarray(sizes, jnp.int32))

    sizes = jnp.where(number % 4 == 0, named(packed, number // 4), named(common, number - number // 4 - 1))
    mixed = jax.random.permutation(jax.random.fold_in(own, 3), number_of)
    source_of, sink = mixed[0:number_of // 2 * 2:2], mixed[1:number_of // 2 * 2:2]
    margin = jnp.minimum(sizes[source_of] - 1, reach - sizes[sink]) // 2
    margin = jnp.where((source_of == sequence[0]) | (sink == sequence[0]) | (sizes[sink] == 0), 0, jnp.maximum(margin, 0))
    shifted = jax.random.randint(jax.random.fold_in(own, 4), (number_of // 2,), 0, 1 << 20) % (margin + 1)
    sizes = sizes.at[source_of].add(-shifted).at[sink].add(shifted)
    items = jnp.searchsorted(jnp.cumsum(sizes), jnp.arange(rows * top), side="right").astype(jnp.int32)
    listing = items.reshape(top, rows).T
    listing = listing[jax.random.permutation(jax.random.fold_in(own, 1), rows)]
    turn = jax.random.randint(jax.random.fold_in(own, 2), (rows, 1), 0, top)
    return jnp.take_along_axis(listing, (jnp.arange(top)[None, :] + turn) % top, axis=1)


def portions_of(amount, total, limit, slope, full):
    portions = [(1 << 20) // math.isqrt(rank ** slope) + 1 for rank in range(1, amount + 1)]
    largest = limit if full else min(limit, max(-(-total // amount), total * portions[0] // sum(portions)))
    least = 1 if total - largest >= amount - 1 else 0
    holding, rest = [largest] + [least] * (amount - 1), total - largest - least * (amount - 1)
    while rest > 0:
        free = [i for i in range(1, amount) if holding[i] < largest] or [i for i in range(1, amount) if holding[i] < limit]
        pool, budget = sum([portions[i] for i in free]), rest
        for i in free:
            extra = min(limit - holding[i], max(1, budget * portions[i] // pool), rest)
            holding[i] = holding[i] + extra
            rest = rest - extra
    return np.array(holding)


def bell_draw(stream_key, shape, deviation, reach, cuts=(), kind=jnp.bfloat16):
    values = deviation * jax.random.normal(stream_key, shape, jnp.float32)
    if cuts:
        values = values * level_of(stream_key, shape, cuts, -0.22, 0.18)
    return jnp.clip(values, -reach, reach).astype(kind)


def setup_inputs(seed: int = 0) -> dict:
    seeds = jax.random.split(jax.random.key(seed), 6)
    volume_sens = bell_draw(seeds[0], (3, NX, NY, NZ), 1.0, 6.0, ((1, 4), (2, 8)), jnp.float32)
    stiffness = draw_stiffness(jax.random.fold_in(seeds[5], 71), 0)
    patch_of_row_keys = jax.random.split(jax.random.fold_in(seeds[2], 1), DEVICES * RS // RS)
    patch_of_row_turns = jax.random.permutation(jax.random.fold_in(seeds[2], 3), DEVICES * RS // RS)
    patch_of_row = jax.vmap(lambda own, number: routed_block(jax.random.fold_in(seeds[2], 2), own, number, RS, PATCHES, 1, CAP, 2))(patch_of_row_keys, patch_of_row_turns).reshape((DEVICES, RS, 1))
    knot_spans = touch_ends(jax.random.randint(seeds[3], (DEVICES, RS, 2), 0, NC - 3), jax.random.fold_in(seeds[3], 1), 0, (NC - 3) - 1).astype(jnp.int32)
    span_params = jnp.clip(1.0 * jax.random.uniform(seeds[4], (DEVICES, RS, 2), jnp.float32) ** level_of(seeds[4], (DEVICES, RS, 2), ((0, 32),), -0.2, 0.2), 0.0, 1.0)
    return {"volume_sens": volume_sens, "stiffness": stiffness, "patch_of_row": patch_of_row, "knot_spans": knot_spans, "span_params": span_params}


omega_relax = 2.0 / 3.0


def six_sides(padded):
    return [padded[..., 2:, 1:-1, 1:-1], padded[..., :-2, 1:-1, 1:-1],
            padded[..., 1:-1, 2:, 1:-1], padded[..., 1:-1, :-2, 1:-1],
            padded[..., 1:-1, 1:-1, 2:], padded[..., 1:-1, 1:-1, :-2]]


def pieces(param):
    other = 1.0 - param
    return [other * other * other / 6.0,
            (3.0 * param ** 3 - 6.0 * param * param + 4.0) / 6.0,
            (-3.0 * param ** 3 + 3.0 * param * param + 3.0 * param + 1.0) / 6.0,
            param ** 3 / 6.0]


def reference(volume_sens, stiffness, patch_of_row, knot_spans, span_params):
    stiff_pad = jnp.pad(stiffness, 1)
    weights = [(stiffness + side) * 0.5 for side in six_sides(stiff_pad)]
    diag = weights[0] + weights[1] + weights[2] + weights[3] + weights[4] + weights[5]
    field = volume_sens
    for sweep in range(SWEEPS):
        scaled = field / diag[None]
        scaled_pad = jnp.pad(scaled, ((0, 0), (1, 1), (1, 1), (1, 1)))
        sides = six_sides(scaled_pad)
        total = jnp.zeros_like(field)
        for index in range(6):
            total = total + weights[index][None] * sides[index]
        field = volume_sens + (1.0 - omega_relax) * field + omega_relax * total
    surface = omega_relax * field[:, :, :, 0] / diag[None, :, :, 0]
    surface = surface.reshape(3, N_GX, CX, N_GY, CY).transpose(0, 1, 3, 2, 4).reshape(3, N_GX * N_GY * RS)
    patch = patch_of_row.reshape(-1).astype(jnp.int32)
    span_a = knot_spans[:, :, 0].reshape(-1).astype(jnp.int32)
    span_e = knot_spans[:, :, 1].reshape(-1).astype(jnp.int32)
    basis_u = pieces(span_params[:, :, 0].reshape(-1))
    basis_v = pieces(span_params[:, :, 1].reshape(-1))
    grads = jnp.zeros((PATCHES, NC, NC, 3), jnp.float32)
    for first in range(4):
        for second in range(4):
            value = (basis_u[first] * basis_v[second])[None] * surface
            grads = grads.at[patch, span_a + first, span_e + second].add(value.T)
    return field, grads.transpose(0, 3, 1, 2)
```

```python
import functools

import jax
import jax.numpy as jnp
from jax import lax
from jax.experimental import pallas as pl
from jax.experimental.pallas import tpu as pltpu
from jax.sharding import PartitionSpec as P

SWEEPS = 3
NC = 64
OMEGA = 2.0 / 3.0
LANES = 128
EDGE = 8
MESH = pl.DeviceIdType.MESH
NT = (((1,), (1,)), ((), ()))


def pieces(param):
    other = 1.0 - param
    square = param * param
    cube = square * param
    return [
        other * other * other / 6.0,
        (3.0 * cube - 6.0 * square + 4.0) / 6.0,
        (-3.0 * cube + 3.0 * square + 3.0 * param + 1.0) / 6.0,
        cube / 6.0,
    ]


def split(values, count):
    parts = []
    for _ in range(count):
        part = values.astype(jnp.bfloat16)
        parts.append(part)
        values = values - part.astype(jnp.float32)
    return parts


def nt_dot(left, right):
    return lax.dot_general(left, right, NT, preferred_element_type=jnp.float32)


def kernel(
    sizes,
    vol_hbm, stiff_hbm, patch_ref, span_ref, param_ref,
    field_hbm, grad_ref,
    vol, cin, cpad, rd, wz, val, y0, y1, y2,
    send1, recv1, csend, crecv, send_y, recv23,
    hot_ref, slot_ref, xcol,
    meta_send, meta_recv, surf_send, surf_recv,
    bu_ref, bvh_ref, bvl_ref,
    in_sem, out_sem, ssem, rsem, cssem, crsem, mssem, mrsem, ussem, ursem,
):
    ngx, ngy, cx, cy, rows = sizes
    n = ngx * ngy
    step = cy + 2 * EDGE
    gx, gy = lax.axis_index("gx"), lax.axis_index("gy")
    me = gx * ngy + gy
    f32, bf16 = jnp.float32, jnp.bfloat16

    load_c = pltpu.make_async_copy(stiff_hbm, cin, in_sem.at[0])
    load_v = pltpu.make_async_copy(vol_hbm, vol, in_sem.at[1])
    load_c.start()
    load_v.start()

    recv1[...] = jnp.zeros(recv1.shape, f32)
    recv23[...] = jnp.zeros(recv23.shape, f32)
    crecv[...] = jnp.zeros(crecv.shape, f32)

    barrier = pltpu.get_barrier_semaphore()

    def greet(i, carry):
        to = lax.rem(me + i, n)
        pl.semaphore_signal(barrier, inc=1, device_id=(to // ngy, lax.rem(to, ngy)), device_id_type=MESH)
        return carry

    lax.fori_loop(1, n, greet, 0)

    def clear(ix, carry):
        base = pl.multiple_of(ix * step, 8)
        for y in (y1, y2):
            y[:, pl.ds(base, EDGE), :] = jnp.zeros((3, EDGE, LANES), f32)
            y[:, pl.ds(base + EDGE + cy, EDGE), :] = jnp.zeros((3, EDGE, LANES), f32)
        return carry

    lax.fori_loop(0, cx + 2, clear, 0)
    for y in (y1, y2):
        y[:, pl.ds(EDGE, cy), :] = jnp.zeros((3, cy, LANES), f32)
        y[:, pl.ds((cx + 1) * step + EDGE, cy), :] = jnp.zeros((3, cy, LANES), f32)

    sides = (
        (gx > 0, (jnp.maximum(gx - 1, 0), gy), 1),
        (gx < ngx - 1, (jnp.minimum(gx + 1, ngx - 1), gy), 0),
        (gy > 0, (gx, jnp.maximum(gy - 1, 0)), 3),
        (gy < ngy - 1, (gx, jnp.minimum(gy + 1, ngy - 1)), 2),
    )

    def face_copy(turn, side, src, dst):
        return pltpu.make_async_remote_copy(
            src_ref=src,
            dst_ref=dst.at[sides[side][2]],
            send_sem=ssem.at[turn * 4 + side],
            recv_sem=rsem.at[turn * 4 + sides[side][2]],
            device_id=sides[side][1],
            device_id_type=MESH,
        )

    def face_wait(turn, side, src, dst):
        return pltpu.make_async_remote_copy(
            src_ref=src,
            dst_ref=dst.at[side],
            send_sem=ssem.at[turn * 4 + side],
            recv_sem=rsem.at[turn * 4 + side],
            device_id=sides[side][1],
            device_id_type=MESH,
        )

    corners = []
    for a in (0, 1):
        for b in (0, 1):
            okay = jnp.logical_and(sides[a][0], sides[2 + b][0])
            corners.append((okay, (sides[a][1][0], sides[2 + b][1][1])))

    def corner_copy(index):
        return pltpu.make_async_remote_copy(
            src_ref=csend.at[index],
            dst_ref=crecv.at[3 - index],
            send_sem=cssem.at[index],
            recv_sem=crsem.at[3 - index],
            device_id=corners[index][1],
            device_id_type=MESH,
        )

    def corner_wait(index):
        return pltpu.make_async_remote_copy(
            src_ref=csend.at[index],
            dst_ref=crecv.at[index],
            send_sem=cssem.at[index],
            recv_sem=crsem.at[index],
            device_id=corners[index][1],
            device_id_type=MESH,
        )

    load_c.wait()
    load_v.wait()
    last = (cx - 1) * cy
    for k in range(3):
        send1[0, k] = vol[k, 0:cy]
        send1[1, k] = vol[k, last:last + cy]
        send1[2, k] = vol[k, pl.ds(0, cx, stride=cy)]
        send1[3, k] = vol[k, pl.ds(cy - 1, cx, stride=cy)]
    for deep in range(2):
        send1[0, 3 + deep] = cin[deep * cy:(deep + 1) * cy]
        send1[1, 3 + deep] = cin[last - deep * cy:last - deep * cy + cy]
        send1[2, 3 + deep] = cin[pl.ds(deep, cx, stride=cy)]
        send1[3, 3 + deep] = cin[pl.ds(cy - 1 - deep, cx, stride=cy)]
    for index in range(4):
        row = (index // 2) * last + (index % 2) * (cy - 1)
        csend[index] = jnp.broadcast_to(cin[row:row + 1], (8, LANES))

    pl.semaphore_wait(barrier, n - 1)
    for side in range(4):
        @pl.when(sides[side][0])
        def _(side=side):
            face_copy(0, side, send1.at[side], recv1).start()
    for index in range(4):
        @pl.when(corners[index][0])
        def _(index=index):
            corner_copy(index).start()

    patch = patch_ref[...]
    hot = (lax.broadcasted_iota(jnp.int32, (n, rows), 0) == patch).astype(f32)
    hot_ref[...] = hot
    upper = (
        lax.broadcasted_iota(jnp.int32, (LANES, LANES), 0)
        <= lax.broadcasted_iota(jnp.int32, (LANES, LANES), 1)
    ).astype(f32).astype(bf16)
    before = jnp.zeros((n, 1), f32)
    for chunk in range(rows // LANES):
        part = hot[:, chunk * LANES:(chunk + 1) * LANES]
        count = jnp.dot(part.astype(bf16), upper, preferred_element_type=f32)
        rank = jnp.sum(part * (count + before), axis=0, keepdims=True) - 1.0
        before = before + count[:, LANES - 1:LANES]
        place = lax.broadcasted_iota(jnp.int32, (LANES, LANES), 0)
        slot_ref[:, chunk * LANES:(chunk + 1) * LANES] = (
            (place == rank.astype(jnp.int32)).astype(f32).astype(bf16)
        )
    hot16 = hot.astype(bf16)
    slots = slot_ref[...]
    for q in range(2):
        total = None
        for part in split(param_ref[q:q + 1, :], 3):
            term = nt_dot(hot16 * part, slots)
            total = term if total is None else total + term
        meta_send[pl.ds(q, n, stride=8), :] = total
        knots = span_ref[q:q + 1, :].astype(f32).astype(bf16)
        meta_send[pl.ds(2 + q, n, stride=8), :] = nt_dot(hot16 * knots, slots)
    meta_send[pl.ds(4, n, stride=8), :] = jnp.zeros((n, LANES), f32)
    meta_send[pl.ds(5, n, stride=8), :] = jnp.zeros((n, LANES), f32)
    meta_send[pl.ds(6, n, stride=8), :] = jnp.zeros((n, LANES), f32)
    meta_send[pl.ds(7, n, stride=8), :] = jnp.zeros((n, LANES), f32)

    def block(number):
        return pl.ds(pl.multiple_of(number * 8, 8), 8)

    def all_copy(src, dst, sems, other, landing):
        return pltpu.make_async_remote_copy(
            src_ref=src.at[block(other)],
            dst_ref=dst.at[block(landing)],
            send_sem=sems[0].at[other],
            recv_sem=sems[1].at[landing],
            device_id=(other // ngy, lax.rem(other, ngy)),
            device_id_type=MESH,
        )

    def send_all(src, dst, sems):
        def go(i, carry):
            all_copy(src, dst, sems, lax.rem(me + i, n), me).start()
            return carry

        lax.fori_loop(1, n, go, 0)
        dst[block(me), :] = src[block(me), :]

    def take_all(src, dst, sems):
        def go(i, carry):
            other = lax.rem(me + i, n)
            all_copy(src, dst, sems, other, other).wait_recv()
            return carry

        lax.fori_loop(1, n, go, 0)

    def sent_all(src, dst, sems):
        def go(i, carry):
            all_copy(src, dst, sems, lax.rem(me + i, n), me).wait_send()
            return carry

        lax.fori_loop(1, n, go, 0)

    meta = (meta_send, meta_recv, (mssem, mrsem))
    surf = (surf_send, surf_recv, (ussem, ursem))
    send_all(*meta)

    def fill(ix, carry):
        to = pl.multiple_of((ix + 2) * step + EDGE, 8)
        cpad[pl.ds(to, cy), :] = cin[pl.ds(pl.multiple_of(ix * cy, 8), cy), :] * (OMEGA / 2)
        return carry

    lax.fori_loop(0, cx, fill, 0)
    for side in range(4):
        @pl.when(sides[side][0])
        def _(side=side):
            face_wait(0, side, send1.at[side], recv1).wait_recv()
    for index in range(4):
        @pl.when(corners[index][0])
        def _(index=index):
            corner_wait(index).wait_recv()
    half = OMEGA / 2
    for deep in range(2):
        low, high = (1 - deep) * step + EDGE, (cx + 2 + deep) * step + EDGE
        cpad[low:low + cy, :] = recv1[0, 3 + deep] * half
        cpad[high:high + cy, :] = recv1[1, 3 + deep] * half
        cpad[pl.ds(2 * step + EDGE - 1 - deep, cx, stride=step), :] = recv1[2, 3 + deep] * half
        cpad[pl.ds(2 * step + EDGE + cy + deep, cx, stride=step), :] = recv1[3, 3 + deep] * half
    for index in range(4):
        row = (1 + (index // 2) * (cx + 1)) * step + EDGE - 1 + (index % 2) * (cy + 1)
        cpad[row:row + 1, :] = crecv[index, 0:1] * half

    def inverse(center, others):
        lane = lax.broadcasted_iota(jnp.int32, center.shape, 1)
        above = jnp.where(lane == LANES - 1, 0.0, pltpu.roll(center, LANES - 1, 1))
        below = jnp.where(lane == 0, 0.0, pltpu.roll(center, 1, 1))
        total = 6.0 * center + above + below
        for other in others:
            total = total + other
        return OMEGA / total, above

    def scale(ix, carry):
        at = pl.multiple_of((ix + 2) * step + EDGE, 8)
        to = pl.multiple_of(ix * cy, 8)
        center = cpad[pl.ds(at, cy), :]
        inv, above = inverse(
            center,
            [cpad[pl.ds(at + d, cy), :] for d in (-step, step, -1, 1)],
        )
        lane = lax.broadcasted_iota(jnp.int32, center.shape, 1)
        rd[pl.ds(to, cy), :] = inv
        wz[pl.ds(to, cy), :] = jnp.where(lane == LANES - 1, 0.0, center + above)
        for k in range(3):
            y0[k, pl.ds(pl.multiple_of(at - step, 8), cy), :] = vol[k, pl.ds(to, cy), :] * inv
        return carry

    lax.fori_loop(0, cx, scale, 0)

    for side in range(4):
        if side < 2:
            at = (1 + side * (cx + 1)) * step + EDGE
            inv, _ = inverse(
                cpad[at:at + cy, :],
                [cpad[at + d:at + d + cy, :] for d in (-step, step, -1, 1)],
            )
            for k in range(3):
                y0[k, at - step + side * 0:at - step + cy, :] = recv1[side, k] * inv
        else:
            at = 2 * step + EDGE - 1 + (side - 2) * (cy + 1)
            inv, _ = inverse(
                cpad[pl.ds(at, cx, stride=step), :],
                [cpad[pl.ds(at + d, cx, stride=step), :] for d in (-step, step, -1, 1)],
            )
            for k in range(3):
                y0[k, pl.ds(at - step, cx, stride=step), :] = recv1[side, k] * inv

    def sweep(vsrc, ysrc, ydst):
        def layer(ix, carry):
            at = pl.multiple_of((ix + 1) * step + EDGE, 8)
            ct = pl.multiple_of((ix + 2) * step + EDGE, 8)
            to = pl.multiple_of(ix * cy, 8)
            center = cpad[pl.ds(ct, cy), :]
            weights = [(d, center + cpad[pl.ds(ct + d, cy), :]) for d in (step, -step, 1, -1)]
            up = wz[pl.ds(to, cy), :]
            inv = rd[pl.ds(to, cy), :]
            for k in range(3):
                mid = ysrc[k, pl.ds(at, cy), :]
                total = up * pltpu.roll(mid, LANES - 1, 1) + pltpu.roll(up * mid, 1, 1)
                for d, weight in weights:
                    total = total + weight * ysrc[k, pl.ds(at + d, cy), :]
                new = vol[k, pl.ds(to, cy), :] + (1.0 - OMEGA) * vsrc[k, pl.ds(to, cy), :] + total
                val[k, pl.ds(to, cy), :] = new
                if ydst is not None:
                    ydst[k, pl.ds(at, cy), :] = new * inv
            return carry

        lax.fori_loop(0, cx, layer, 0)

    def send_faces(turn, y):
        low, high = step + EDGE, cx * step + EDGE
        for k in range(3):
            send_y[turn - 1, 2, k] = y[k, pl.ds(low, cx, stride=step), :]
            send_y[turn - 1, 3, k] = y[k, pl.ds(low + cy - 1, cx, stride=step), :]
            send_y[turn - 1, 0, k] = y[k, low:low + cy, :]
            send_y[turn - 1, 1, k] = y[k, high:high + cy, :]
        for side in range(4):
            @pl.when(sides[side][0])
            def _(side=side):
                face_copy(turn, side, send_y.at[turn - 1, side], recv23.at[turn - 1]).start()

    def add_faces(turn, ydst):
        for side in range(4):
            @pl.when(sides[side][0])
            def _(side=side):
                face_wait(turn, side, send_y.at[turn - 1, side], recv23.at[turn - 1]).wait_recv()
        for side in range(4):
            if side < 2:
                ct = (2 + side * (cx - 1)) * step + EDGE
                to = side * last
                outer = ct + (step if side else -step)
                here, there, flat = pl.ds(ct, cy), pl.ds(outer, cy), pl.ds(to, cy)
                pad = pl.ds(ct - step, cy)
            else:
                shift = (side - 2) * (cy - 1)
                ct = 2 * step + EDGE + shift
                outer = ct + (1 if side == 3 else -1)
                here, there = pl.ds(ct, cx, stride=step), pl.ds(outer, cx, stride=step)
                flat = pl.ds(shift, cx, stride=cy)
                pad = pl.ds(ct - step, cx, stride=step)
            weight = cpad[here, :] + cpad[there, :]
            inv = rd[flat, :]
            for k in range(3):
                more = weight * recv23[turn - 1, side, k]
                val[k, flat, :] = val[k, flat, :] + more
                if ydst is not None:
                    ydst[k, pad, :] = ydst[k, pad, :] + more * inv

    sweep(vol, y0, y1)
    send_faces(1, y1)
    sweep(val, y1, y2)
    add_faces(1, y2)
    send_faces(2, y2)
    sweep(val, y2, None)

    take_all(*meta)
    basis_u = pieces(meta_recv[pl.ds(0, n, stride=8), :])
    basis_v = pieces(meta_recv[pl.ds(1, n, stride=8), :])
    span_u = meta_recv[pl.ds(2, n, stride=8), :].astype(jnp.int32)
    span_v = meta_recv[pl.ds(3, n, stride=8), :].astype(jnp.int32)
    knot = lax.broadcasted_iota(jnp.int32, (NC, LANES), 0)

    def spline(span, basis, d):
        offset = knot - span[d:d + 1, :]
        out = jnp.where(offset == 0, basis[0][d:d + 1, :], 0.0)
        for index in range(1, 4):
            out = jnp.where(offset == index, basis[index][d:d + 1, :], out)
        return out

    for d in range(n):
        lanes = slice(d * LANES, (d + 1) * LANES)
        bu_ref[:, lanes] = spline(span_u, basis_u, d)
        high, low = split(spline(span_v, basis_v, d), 2)
        bvh_ref[:, lanes] = high
        bvl_ref[:, lanes] = low

    add_faces(2, None)
    store = pltpu.make_async_copy(val, field_hbm, out_sem)
    store.start()

    def surface(ix, carry):
        to = pl.ds(pl.multiple_of(ix * cy, 8), cy)
        lane = lax.broadcasted_iota(jnp.int32, (cy, LANES), 1)
        inv = rd[to, :] * OMEGA
        out = jnp.where(lane == 0, val[0, to, :] * inv, 0.0)
        for k in (1, 2):
            out = jnp.where(lane == k, pltpu.roll(val[k, to, :] * inv, k, 1), out)
        xcol[to, :] = out
        return carry

    lax.fori_loop(0, cx, surface, 0)
    surf_rows = jnp.concatenate(
        [xcol[c * LANES:(c + 1) * LANES, :].T[0:8] for c in range(rows // LANES)], axis=1
    )
    hot16 = hot_ref[...].astype(bf16)
    slots = slot_ref[...]
    for k in range(3):
        total = None
        for part in split(surf_rows[k:k + 1, :], 3):
            term = nt_dot(hot16 * part, slots)
            total = term if total is None else total + term
        surf_send[pl.ds(k, n, stride=8), :] = total
    for k in range(3, 8):
        surf_send[pl.ds(k, n, stride=8), :] = jnp.zeros((n, LANES), f32)
    send_all(*surf)
    take_all(*surf)

    group = 8
    total = jnp.zeros((3 * NC, NC), f32)
    for first in range(0, n, group):
        lanes = slice(first * LANES, (first + group) * LANES)
        bu = bu_ref[:, lanes]
        left = jnp.concatenate(
            [
                bu * jnp.concatenate(
                    [surf_recv[d * 8 + k:d * 8 + k + 1, :] for d in range(first, first + group)],
                    axis=1,
                )
                for k in range(3)
            ],
            axis=0,
        )
        high, low = split(left, 2)
        bvh = bvh_ref[:, lanes]
        total = total + nt_dot(high, bvh) + nt_dot(low, bvh) + nt_dot(high, bvl_ref[:, lanes])
    for k in range(3):
        grad_ref[k] = total[k * NC:(k + 1) * NC]

    for side in range(4):
        @pl.when(sides[side][0])
        def _(side=side):
            face_copy(0, side, send1.at[side], recv1).wait_send()
            for turn in (1, 2):
                face_copy(turn, side, send_y.at[turn - 1, side], recv23.at[turn - 1]).wait_send()
    for index in range(4):
        @pl.when(corners[index][0])
        def _(index=index):
            corner_copy(index).wait_send()
    sent_all(*meta)
    sent_all(*surf)
    store.wait()


def body(volume_sens, stiffness, patch_of_row, knot_spans, span_params):
    ngx, ngy = lax.axis_size("gx"), lax.axis_size("gy")
    n = ngx * ngy
    _, cx, cy, nz = volume_sens.shape
    rows = cx * cy
    step = cy + 2 * EDGE
    f32, bf16 = jnp.float32, jnp.bfloat16
    dma = pltpu.SemaphoreType.DMA
    field, grads = pl.pallas_call(
        functools.partial(kernel, (ngx, ngy, cx, cy, rows)),
        out_shape=(
            jax.ShapeDtypeStruct((3, rows, nz), f32),
            jax.ShapeDtypeStruct((3, NC, NC), f32),
        ),
        in_specs=[
            pl.BlockSpec(memory_space=pl.ANY),
            pl.BlockSpec(memory_space=pl.ANY),
            pl.BlockSpec(memory_space=pltpu.VMEM),
            pl.BlockSpec(memory_space=pltpu.VMEM),
            pl.BlockSpec(memory_space=pltpu.VMEM),
        ],
        out_specs=(
            pl.BlockSpec(memory_space=pl.ANY),
            pl.BlockSpec(memory_space=pltpu.VMEM),
        ),
        scratch_shapes=[
            pltpu.VMEM((3, rows, nz), f32),
            pltpu.VMEM((rows, nz), f32),
            pltpu.VMEM(((cx + 4) * step, nz), f32),
            pltpu.VMEM((rows, nz), f32),
            pltpu.VMEM((rows, nz), f32),
            pltpu.VMEM((3, rows, nz), f32),
            pltpu.VMEM((3, (cx + 2) * step, nz), f32),
            pltpu.VMEM((3, (cx + 2) * step, nz), f32),
            pltpu.VMEM((3, (cx + 2) * step, nz), f32),
            pltpu.VMEM((4, 5, cy, nz), f32),
            pltpu.VMEM((4, 5, cy, nz), f32),
            pltpu.VMEM((4, 8, nz), f32),
            pltpu.VMEM((4, 8, nz), f32),
            pltpu.VMEM((2, 4, 3, cy, nz), f32),
            pltpu.VMEM((2, 4, 3, cy, nz), f32),
            pltpu.VMEM((n, rows), f32),
            pltpu.VMEM((LANES, rows), bf16),
            pltpu.VMEM((rows, nz), f32),
            pltpu.VMEM((n * 8, LANES), f32),
            pltpu.VMEM((n * 8, LANES), f32),
            pltpu.VMEM((n * 8, LANES), f32),
            pltpu.VMEM((n * 8, LANES), f32),
            pltpu.VMEM((NC, n * LANES), f32),
            pltpu.VMEM((NC, n * LANES), bf16),
            pltpu.VMEM((NC, n * LANES), bf16),
            dma((2,)),
            dma,
            dma((12,)),
            dma((12,)),
            dma((4,)),
            dma((4,)),
            dma((n,)),
            dma((n,)),
            dma((n,)),
            dma((n,)),
        ],
        compiler_params=pltpu.CompilerParams(
            collective_id=0, has_side_effects=True, vmem_limit_bytes=56 * 2**20
        ),
    )(
        volume_sens.reshape(3, rows, nz),
        stiffness.reshape(rows, nz),
        patch_of_row.reshape(1, rows),
        knot_spans[0].T,
        span_params[0].T,
    )
    return field.reshape(volume_sens.shape), grads[None]


def solution(mesh):
    placed = (
        P(None, "gx", "gy", None),
        P("gx", "gy", None),
        P(("gx", "gy"), None, None),
        P(("gx", "gy"), None, None),
        P(("gx", "gy"), None, None),
    )
    return jax.shard_map(
        body,
        mesh=mesh,
        in_specs=placed,
        out_specs=(P(None, "gx", "gy", None), P(("gx", "gy"), None, None, None)),
        check_vma=False,
    )
```

```python
import functools

import jax
import jax.numpy as jnp
from jax import lax
from jax.experimental import pallas as pl
from jax.experimental.pallas import tpu as pltpu
from jax.sharding import PartitionSpec as P

SWEEPS = 3
NC = 64
OMEGA = 2.0 / 3.0
LANES = 128
EDGE = 8
UNROLL = 4
MESH = pl.DeviceIdType.MESH
NT = (((1,), (1,)), ((), ()))


def pieces(param):
    other = 1.0 - param
    square = param * param
    cube = square * param
    return [
        other * other * other / 6.0,
        (3.0 * cube - 6.0 * square + 4.0) / 6.0,
        (-3.0 * cube + 3.0 * square + 3.0 * param + 1.0) / 6.0,
        cube / 6.0,
    ]


def split(values, count):
    parts = []
    for _ in range(count):
        part = values.astype(jnp.bfloat16)
        parts.append(part)
        values = values - part.astype(jnp.float32)
    return parts


def nt_dot(left, right):
    return lax.dot_general(left, right, NT, preferred_element_type=jnp.float32)


def kernel(
    sizes,
    vol_hbm, stiff_hbm, patch_ref, span_ref, param_ref,
    field, grad_ref,
    vol, cin, cpad, rd, wz, val, y0, y1, y2,
    send1, recv1, csend, crecv, send_y, recv23,
    hot_ref, slot_ref, xcol,
    meta_send, meta_recv, surf_send, surf_recv,
    bu_ref, bv_ref,
    in_sem, ssem, rsem, cssem, crsem, mssem, mrsem, ussem, ursem,
):
    ngx, ngy, cx, cy, rows = sizes
    n = ngx * ngy
    step = cy + 2 * EDGE
    gx, gy = lax.axis_index("gx"), lax.axis_index("gy")
    me = gx * ngy + gy
    f32, bf16 = jnp.float32, jnp.bfloat16

    load_c = pltpu.make_async_copy(stiff_hbm, cin, in_sem.at[0])
    load_v = pltpu.make_async_copy(vol_hbm, vol, in_sem.at[1])
    load_c.start()
    load_v.start()

    recv1[...] = jnp.zeros(recv1.shape, f32)
    recv23[...] = jnp.zeros(recv23.shape, f32)
    crecv[...] = jnp.zeros(crecv.shape, f32)

    barrier = pltpu.get_barrier_semaphore()

    def greet(i, carry):
        to = lax.rem(me + i, n)
        pl.semaphore_signal(barrier, inc=1, device_id=(to // ngy, lax.rem(to, ngy)), device_id_type=MESH)
        return carry

    lax.fori_loop(1, n, greet, 0)

    def clear(ix, carry):
        base = pl.multiple_of(ix * step, 8)
        for y in (y1, y2):
            y[:, pl.ds(base, EDGE), :] = jnp.zeros((3, EDGE, LANES), f32)
            y[:, pl.ds(base + EDGE + cy, EDGE), :] = jnp.zeros((3, EDGE, LANES), f32)
        return carry

    lax.fori_loop(0, cx + 2, clear, 0)
    for y in (y1, y2):
        y[:, pl.ds(EDGE, cy), :] = jnp.zeros((3, cy, LANES), f32)
        y[:, pl.ds((cx + 1) * step + EDGE, cy), :] = jnp.zeros((3, cy, LANES), f32)

    sides = (
        (gx > 0, (jnp.maximum(gx - 1, 0), gy), 1),
        (gx < ngx - 1, (jnp.minimum(gx + 1, ngx - 1), gy), 0),
        (gy > 0, (gx, jnp.maximum(gy - 1, 0)), 3),
        (gy < ngy - 1, (gx, jnp.minimum(gy + 1, ngy - 1)), 2),
    )

    def face_copy(turn, side, src, dst):
        return pltpu.make_async_remote_copy(
            src_ref=src,
            dst_ref=dst.at[sides[side][2]],
            send_sem=ssem.at[turn * 4 + side],
            recv_sem=rsem.at[turn * 4 + sides[side][2]],
            device_id=sides[side][1],
            device_id_type=MESH,
        )

    def face_wait(turn, side, src, dst):
        return pltpu.make_async_remote_copy(
            src_ref=src,
            dst_ref=dst.at[side],
            send_sem=ssem.at[turn * 4 + side],
            recv_sem=rsem.at[turn * 4 + side],
            device_id=sides[side][1],
            device_id_type=MESH,
        )

    corners = []
    for a in (0, 1):
        for b in (0, 1):
            okay = jnp.logical_and(sides[a][0], sides[2 + b][0])
            corners.append((okay, (sides[a][1][0], sides[2 + b][1][1])))

    def corner_copy(index):
        return pltpu.make_async_remote_copy(
            src_ref=csend.at[index],
            dst_ref=crecv.at[3 - index],
            send_sem=cssem.at[index],
            recv_sem=crsem.at[3 - index],
            device_id=corners[index][1],
            device_id_type=MESH,
        )

    def corner_wait(index):
        return pltpu.make_async_remote_copy(
            src_ref=csend.at[index],
            dst_ref=crecv.at[index],
            send_sem=cssem.at[index],
            recv_sem=crsem.at[index],
            device_id=corners[index][1],
            device_id_type=MESH,
        )

    load_c.wait()
    load_v.wait()
    last = (cx - 1) * cy
    for k in range(3):
        send1[0, k] = vol[k, 0:cy]
        send1[1, k] = vol[k, last:last + cy]
        send1[2, k] = vol[k, pl.ds(0, cx, stride=cy)]
        send1[3, k] = vol[k, pl.ds(cy - 1, cx, stride=cy)]
    for deep in range(2):
        send1[0, 3 + deep] = cin[deep * cy:(deep + 1) * cy]
        send1[1, 3 + deep] = cin[last - deep * cy:last - deep * cy + cy]
        send1[2, 3 + deep] = cin[pl.ds(deep, cx, stride=cy)]
        send1[3, 3 + deep] = cin[pl.ds(cy - 1 - deep, cx, stride=cy)]
    for index in range(4):
        row = (index // 2) * last + (index % 2) * (cy - 1)
        csend[index] = jnp.broadcast_to(cin[row:row + 1], (8, LANES))

    pl.semaphore_wait(barrier, n - 1)
    for side in range(4):
        @pl.when(sides[side][0])
        def _(side=side):
            face_copy(0, side, send1.at[side], recv1).start()
    for index in range(4):
        @pl.when(corners[index][0])
        def _(index=index):
            corner_copy(index).start()

    patch = patch_ref[...]
    hot = (lax.broadcasted_iota(jnp.int32, (n, rows), 0) == patch).astype(f32)
    hot_ref[...] = hot
    upper = (
        lax.broadcasted_iota(jnp.int32, (LANES, LANES), 0)
        <= lax.broadcasted_iota(jnp.int32, (LANES, LANES), 1)
    ).astype(f32).astype(bf16)
    before = jnp.zeros((n, 1), f32)
    for chunk in range(rows // LANES):
        part = hot[:, chunk * LANES:(chunk + 1) * LANES]
        count = jnp.dot(part.astype(bf16), upper, preferred_element_type=f32)
        rank = jnp.sum(part * (count + before), axis=0, keepdims=True) - 1.0
        before = before + count[:, LANES - 1:LANES]
        place = lax.broadcasted_iota(jnp.int32, (LANES, LANES), 0)
        slot_ref[:, chunk * LANES:(chunk + 1) * LANES] = (
            (place == rank.astype(jnp.int32)).astype(f32).astype(bf16)
        )
    hot16 = hot.astype(bf16)
    slots = slot_ref[...]
    stack = []
    for q in range(2):
        stack += split(param_ref[q:q + 1, :], 3)
    for q in range(2):
        stack.append(span_ref[q:q + 1, :].astype(f32).astype(bf16))
    out = nt_dot(jnp.concatenate([hot16 * part for part in stack], axis=0), slots)
    out = [out[i * n:(i + 1) * n] for i in range(8)]
    meta_send[pl.ds(0, n, stride=8), :] = out[0] + out[1] + out[2]
    meta_send[pl.ds(1, n, stride=8), :] = out[3] + out[4] + out[5]
    meta_send[pl.ds(2, n, stride=8), :] = out[6]
    meta_send[pl.ds(3, n, stride=8), :] = out[7]
    meta_send[pl.ds(4, n, stride=8), :] = jnp.zeros((n, LANES), f32)
    meta_send[pl.ds(5, n, stride=8), :] = jnp.zeros((n, LANES), f32)
    meta_send[pl.ds(6, n, stride=8), :] = jnp.zeros((n, LANES), f32)
    meta_send[pl.ds(7, n, stride=8), :] = jnp.zeros((n, LANES), f32)

    def block(number):
        return pl.ds(pl.multiple_of(number * 8, 8), 8)

    def all_copy(src, dst, sems, other, landing):
        return pltpu.make_async_remote_copy(
            src_ref=src.at[block(other)],
            dst_ref=dst.at[block(landing)],
            send_sem=sems[0].at[other],
            recv_sem=sems[1].at[landing],
            device_id=(other // ngy, lax.rem(other, ngy)),
            device_id_type=MESH,
        )

    def send_all(src, dst, sems):
        def go(i, carry):
            all_copy(src, dst, sems, lax.rem(me + i, n), me).start()
            return carry

        lax.fori_loop(1, n, go, 0)
        dst[block(me), :] = src[block(me), :]

    def take_all(src, dst, sems):
        def go(i, carry):
            other = lax.rem(me + i, n)
            all_copy(src, dst, sems, other, other).wait_recv()
            return carry

        lax.fori_loop(1, n, go, 0)

    def sent_all(src, dst, sems):
        def go(i, carry):
            all_copy(src, dst, sems, lax.rem(me + i, n), me).wait_send()
            return carry

        lax.fori_loop(1, n, go, 0)

    meta = (meta_send, meta_recv, (mssem, mrsem))
    surf = (surf_send, surf_recv, (ussem, ursem))
    send_all(*meta)

    def fill(ix, carry):
        to = pl.multiple_of((ix + 2) * step + EDGE, 8)
        cpad[pl.ds(to, cy), :] = cin[pl.ds(pl.multiple_of(ix * cy, 8), cy), :] * (OMEGA / 2)
        return carry

    lax.fori_loop(0, cx, fill, 0, unroll=UNROLL)
    for side in range(4):
        @pl.when(sides[side][0])
        def _(side=side):
            face_wait(0, side, send1.at[side], recv1).wait_recv()
    for index in range(4):
        @pl.when(corners[index][0])
        def _(index=index):
            corner_wait(index).wait_recv()
    half = OMEGA / 2
    for deep in range(2):
        low, high = (1 - deep) * step + EDGE, (cx + 2 + deep) * step + EDGE
        cpad[low:low + cy, :] = recv1[0, 3 + deep] * half
        cpad[high:high + cy, :] = recv1[1, 3 + deep] * half
        cpad[pl.ds(2 * step + EDGE - 1 - deep, cx, stride=step), :] = recv1[2, 3 + deep] * half
        cpad[pl.ds(2 * step + EDGE + cy + deep, cx, stride=step), :] = recv1[3, 3 + deep] * half
    for index in range(4):
        row = (1 + (index // 2) * (cx + 1)) * step + EDGE - 1 + (index % 2) * (cy + 1)
        cpad[row:row + 1, :] = crecv[index, 0:1] * half

    def inverse(center, others):
        lane = lax.broadcasted_iota(jnp.int32, center.shape, 1)
        above = jnp.where(lane == LANES - 1, 0.0, pltpu.roll(center, LANES - 1, 1))
        below = jnp.where(lane == 0, 0.0, pltpu.roll(center, 1, 1))
        total = 6.0 * center + above + below
        for other in others:
            total = total + other
        return OMEGA / total, above

    def scale(it, carry):
        done = []
        for u in range(UNROLL):
            ix = it * UNROLL + u
            at = pl.multiple_of((ix + 2) * step + EDGE, 8)
            to = pl.multiple_of(ix * cy, 8)
            center = cpad[pl.ds(at, cy), :]
            inv, above = inverse(
                center,
                [cpad[pl.ds(at + d, cy), :] for d in (-step, step, -1, 1)],
            )
            lane = lax.broadcasted_iota(jnp.int32, center.shape, 1)
            up = jnp.where(lane == LANES - 1, 0.0, center + above)
            done.append((at, to, inv, up, vol[:, pl.ds(to, cy), :] * inv[None]))
        for at, to, inv, up, scaled in done:
            rd[pl.ds(to, cy), :] = inv
            wz[pl.ds(to, cy), :] = up
            y0[:, pl.ds(pl.multiple_of(at - step, 8), cy), :] = scaled
        return carry

    lax.fori_loop(0, cx // UNROLL, scale, 0)

    for side in range(4):
        if side < 2:
            at = (1 + side * (cx + 1)) * step + EDGE
            inv, _ = inverse(
                cpad[at:at + cy, :],
                [cpad[at + d:at + d + cy, :] for d in (-step, step, -1, 1)],
            )
            for k in range(3):
                y0[k, at - step + side * 0:at - step + cy, :] = recv1[side, k] * inv
        else:
            at = 2 * step + EDGE - 1 + (side - 2) * (cy + 1)
            inv, _ = inverse(
                cpad[pl.ds(at, cx, stride=step), :],
                [cpad[pl.ds(at + d, cx, stride=step), :] for d in (-step, step, -1, 1)],
            )
            for k in range(3):
                y0[k, pl.ds(at - step, cx, stride=step), :] = recv1[side, k] * inv

    def sweep(vsrc, vdst, ysrc, ydst):
        def layers(it, carry):
            done = []
            for u in range(UNROLL):
                ix = it * UNROLL + u
                at = pl.multiple_of((ix + 1) * step + EDGE, 8)
                ct = pl.multiple_of((ix + 2) * step + EDGE, 8)
                to = pl.multiple_of(ix * cy, 8)
                center = cpad[pl.ds(ct, cy), :]
                up = wz[pl.ds(to, cy), :][None]
                mid = ysrc[:, pl.ds(at, cy), :]
                total = up * pltpu.roll(mid, LANES - 1, 2) + pltpu.roll(up * mid, 1, 2)
                for d in (step, -step, 1, -1):
                    weight = center + cpad[pl.ds(ct + d, cy), :]
                    total = total + weight[None] * ysrc[:, pl.ds(at + d, cy), :]
                new = vol[:, pl.ds(to, cy), :] + (1.0 - OMEGA) * vsrc[:, pl.ds(to, cy), :] + total
                done.append((at, to, new))
            for at, to, new in done:
                vdst[:, pl.ds(to, cy), :] = new
                if ydst is not None:
                    ydst[:, pl.ds(at, cy), :] = new * rd[pl.ds(to, cy), :][None]
            return carry

        lax.fori_loop(0, cx // UNROLL, layers, 0)

    def send_faces(turn, y):
        low, high = step + EDGE, cx * step + EDGE
        for k in range(3):
            send_y[turn - 1, 2, k] = y[k, pl.ds(low, cx, stride=step), :]
            send_y[turn - 1, 3, k] = y[k, pl.ds(low + cy - 1, cx, stride=step), :]
            send_y[turn - 1, 0, k] = y[k, low:low + cy, :]
            send_y[turn - 1, 1, k] = y[k, high:high + cy, :]
        for side in range(4):
            @pl.when(sides[side][0])
            def _(side=side):
                face_copy(turn, side, send_y.at[turn - 1, side], recv23.at[turn - 1]).start()

    def add_faces(turn, val, ydst):
        for side in range(4):
            @pl.when(sides[side][0])
            def _(side=side):
                face_wait(turn, side, send_y.at[turn - 1, side], recv23.at[turn - 1]).wait_recv()
        for side in range(4):
            if side < 2:
                ct = (2 + side * (cx - 1)) * step + EDGE
                to = side * last
                outer = ct + (step if side else -step)
                here, there, flat = pl.ds(ct, cy), pl.ds(outer, cy), pl.ds(to, cy)
                pad = pl.ds(ct - step, cy)
            else:
                shift = (side - 2) * (cy - 1)
                ct = 2 * step + EDGE + shift
                outer = ct + (1 if side == 3 else -1)
                here, there = pl.ds(ct, cx, stride=step), pl.ds(outer, cx, stride=step)
                flat = pl.ds(shift, cx, stride=cy)
                pad = pl.ds(ct - step, cx, stride=step)
            weight = cpad[here, :] + cpad[there, :]
            inv = rd[flat, :]
            for k in range(3):
                more = weight * recv23[turn - 1, side, k]
                val[k, flat, :] = val[k, flat, :] + more
                if ydst is not None:
                    ydst[k, pad, :] = ydst[k, pad, :] + more * inv

    sweep(vol, field, y0, y1)
    send_faces(1, y1)
    sweep(field, val, y1, y2)
    add_faces(1, val, y2)
    send_faces(2, y2)
    sweep(val, field, y2, None)

    take_all(*meta)
    basis_u = pieces(meta_recv[pl.ds(0, n, stride=8), :])
    basis_v = pieces(meta_recv[pl.ds(1, n, stride=8), :])
    span_u = meta_recv[pl.ds(2, n, stride=8), :].astype(jnp.int32)
    span_v = meta_recv[pl.ds(3, n, stride=8), :].astype(jnp.int32)
    knot = lax.broadcasted_iota(jnp.int32, (NC, LANES), 0)

    def spline(span, basis, d):
        offset = knot - span[d:d + 1, :]
        out = jnp.where(offset == 0, basis[0][d:d + 1, :], 0.0)
        for index in range(1, 4):
            out = jnp.where(offset == index, basis[index][d:d + 1, :], out)
        return out

    for d in range(n):
        lanes = slice(d * LANES, (d + 1) * LANES)
        bu_ref[:, lanes] = spline(span_u, basis_u, d)
        high, low = split(spline(span_v, basis_v, d), 2)
        bv_ref[:NC, lanes] = high
        bv_ref[NC:, lanes] = low

    add_faces(2, field, None)

    def surface(ix, carry):
        to = pl.ds(pl.multiple_of(ix * cy, 8), cy)
        lane = lax.broadcasted_iota(jnp.int32, (cy, LANES), 1)
        inv = rd[to, :] * OMEGA
        out = jnp.where(lane == 0, field[0, to, :] * inv, 0.0)
        for k in (1, 2):
            out = jnp.where(lane == k, pltpu.roll(field[k, to, :] * inv, k, 1), out)
        xcol[to, :] = out
        return carry

    lax.fori_loop(0, cx, surface, 0, unroll=UNROLL)
    surf_rows = jnp.concatenate(
        [xcol[c * LANES:(c + 1) * LANES, :].T[0:8] for c in range(rows // LANES)], axis=1
    )
    hot16 = hot_ref[...].astype(bf16)
    slots = slot_ref[...]
    stack = []
    for k in range(3):
        stack += split(surf_rows[k:k + 1, :], 3)
    out = nt_dot(jnp.concatenate([hot16 * part for part in stack], axis=0), slots)
    out = [out[i * n:(i + 1) * n] for i in range(9)]
    for k in range(3):
        surf_send[pl.ds(k, n, stride=8), :] = out[3 * k] + out[3 * k + 1] + out[3 * k + 2]
    for k in range(3, 8):
        surf_send[pl.ds(k, n, stride=8), :] = jnp.zeros((n, LANES), f32)
    send_all(*surf)
    take_all(*surf)

    group = 8
    total = jnp.zeros((6 * NC, 2 * NC), f32)
    for first in range(0, n, group):
        lanes = slice(first * LANES, (first + group) * LANES)
        bu = bu_ref[:, lanes]
        left = jnp.concatenate(
            [
                bu * jnp.concatenate(
                    [surf_recv[d * 8 + k:d * 8 + k + 1, :] for d in range(first, first + group)],
                    axis=1,
                )
                for k in range(3)
            ],
            axis=0,
        )
        total = total + nt_dot(jnp.concatenate(split(left, 2), axis=0), bv_ref[:, lanes])
    for k in range(3):
        high, low = total[k * NC:(k + 1) * NC], total[(3 + k) * NC:(4 + k) * NC]
        grad_ref[k] = high[:, :NC] + high[:, NC:] + low[:, :NC] + low[:, NC:]

    for side in range(4):
        @pl.when(sides[side][0])
        def _(side=side):
            face_copy(0, side, send1.at[side], recv1).wait_send()
            for turn in (1, 2):
                face_copy(turn, side, send_y.at[turn - 1, side], recv23.at[turn - 1]).wait_send()
    for index in range(4):
        @pl.when(corners[index][0])
        def _(index=index):
            corner_copy(index).wait_send()
    sent_all(*meta)
    sent_all(*surf)


def body(volume_sens, stiffness, patch_of_row, knot_spans, span_params):
    ngx, ngy = lax.axis_size("gx"), lax.axis_size("gy")
    n = ngx * ngy
    _, cx, cy, nz = volume_sens.shape
    rows = cx * cy
    step = cy + 2 * EDGE
    f32, bf16 = jnp.float32, jnp.bfloat16
    dma = pltpu.SemaphoreType.DMA
    field, grads = pl.pallas_call(
        functools.partial(kernel, (ngx, ngy, cx, cy, rows)),
        out_shape=(
            pltpu.VMEM((3, rows, nz), f32),
            pltpu.VMEM((3, NC, NC), f32),
        ),
        in_specs=[
            pl.BlockSpec(memory_space=pl.ANY),
            pl.BlockSpec(memory_space=pl.ANY),
            pl.BlockSpec(memory_space=pltpu.VMEM),
            pl.BlockSpec(memory_space=pltpu.VMEM),
            pl.BlockSpec(memory_space=pltpu.VMEM),
        ],
        out_specs=(
            pl.BlockSpec(memory_space=pltpu.VMEM),
            pl.BlockSpec(memory_space=pltpu.VMEM),
        ),
        scratch_shapes=[
            pltpu.VMEM((3, rows, nz), f32),
            pltpu.VMEM((rows, nz), f32),
            pltpu.VMEM(((cx + 4) * step, nz), f32),
            pltpu.VMEM((rows, nz), f32),
            pltpu.VMEM((rows, nz), f32),
            pltpu.VMEM((3, rows, nz), f32),
            pltpu.VMEM((3, (cx + 2) * step, nz), f32),
            pltpu.VMEM((3, (cx + 2) * step, nz), f32),
            pltpu.VMEM((3, (cx + 2) * step, nz), f32),
            pltpu.VMEM((4, 5, cy, nz), f32),
            pltpu.VMEM((4, 5, cy, nz), f32),
            pltpu.VMEM((4, 8, nz), f32),
            pltpu.VMEM((4, 8, nz), f32),
            pltpu.VMEM((2, 4, 3, cy, nz), f32),
            pltpu.VMEM((2, 4, 3, cy, nz), f32),
            pltpu.VMEM((n, rows), f32),
            pltpu.VMEM((LANES, rows), bf16),
            pltpu.VMEM((rows, nz), f32),
            pltpu.VMEM((n * 8, LANES), f32),
            pltpu.VMEM((n * 8, LANES), f32),
            pltpu.VMEM((n * 8, LANES), f32),
            pltpu.VMEM((n * 8, LANES), f32),
            pltpu.VMEM((NC, n * LANES), f32),
            pltpu.VMEM((2 * NC, n * LANES), bf16),
            dma((2,)),
            dma((12,)),
            dma((12,)),
            dma((4,)),
            dma((4,)),
            dma((n,)),
            dma((n,)),
            dma((n,)),
            dma((n,)),
        ],
        compiler_params=pltpu.CompilerParams(
            collective_id=0, has_side_effects=True, vmem_limit_bytes=56 * 2**20
        ),
    )(
        volume_sens.reshape(3, rows, nz),
        stiffness.reshape(rows, nz),
        patch_of_row.reshape(1, rows),
        knot_spans[0].T,
        span_params[0].T,
    )
    return field.reshape(volume_sens.shape), grads[None]


def solution(mesh):
    placed = (
        P(None, "gx", "gy", None),
        P("gx", "gy", None),
        P(("gx", "gy"), None, None),
        P(("gx", "gy"), None, None),
        P(("gx", "gy"), None, None),
    )
    return jax.shard_map(
        body,
        mesh=mesh,
        in_specs=placed,
        out_specs=(P(None, "gx", "gy", None), P(("gx", "gy"), None, None, None)),
        check_vma=False,
    )
```

```python
import functools

import jax
import jax.numpy as jnp
from jax import lax
from jax.experimental import pallas as pl
from jax.experimental.pallas import tpu as pltpu
from jax.sharding import PartitionSpec as P

SWEEPS = 3
NC = 64
OMEGA = 2.0 / 3.0
LANES = 128
EDGE = 8
UNROLL = 4
MESH = pl.DeviceIdType.MESH
NT = (((1,), (1,)), ((), ()))


def pieces(param):
    other = 1.0 - param
    square = param * param
    cube = square * param
    return [
        other * other * other / 6.0,
        (3.0 * cube - 6.0 * square + 4.0) / 6.0,
        (-3.0 * cube + 3.0 * square + 3.0 * param + 1.0) / 6.0,
        cube / 6.0,
    ]


def split(values, count):
    parts = []
    for _ in range(count):
        part = values.astype(jnp.bfloat16)
        parts.append(part)
        values = values - part.astype(jnp.float32)
    return parts


def nt_dot(left, right):
    return lax.dot_general(left, right, NT, preferred_element_type=jnp.float32)


def kernel(
    sizes,
    vol_hbm, stiff_hbm, patch_ref, span_ref, param_ref,
    field, surf_recv, bu_ref, bv_ref,
    vol, cin, cpad, rd, wz, val, y0, y1, y2,
    send1, recv1, csend, crecv, send_y, recv23,
    hot_ref, slot_ref, xcol,
    meta_send, meta_recv, surf_send,
    in_sem, ssem, rsem, cssem, crsem, mssem, mrsem, ussem, ursem,
):
    ngx, ngy, cx, cy, rows = sizes
    n = ngx * ngy
    step = cy + 2 * EDGE
    gx, gy = lax.axis_index("gx"), lax.axis_index("gy")
    me = gx * ngy + gy
    f32, bf16 = jnp.float32, jnp.bfloat16

    load_c = pltpu.make_async_copy(stiff_hbm, cin, in_sem.at[0])
    load_v = pltpu.make_async_copy(vol_hbm, vol, in_sem.at[1])
    load_c.start()
    load_v.start()

    barrier = pltpu.get_barrier_semaphore()

    def greet(i, carry):
        to = lax.rem(me + i, n)
        pl.semaphore_signal(barrier, inc=1, device_id=(to // ngy, lax.rem(to, ngy)), device_id_type=MESH)
        return carry

    lax.fori_loop(1, n, greet, 0)

    sides = (
        (gx > 0, (jnp.maximum(gx - 1, 0), gy), 1),
        (gx < ngx - 1, (jnp.minimum(gx + 1, ngx - 1), gy), 0),
        (gy > 0, (gx, jnp.maximum(gy - 1, 0)), 3),
        (gy < ngy - 1, (gx, jnp.minimum(gy + 1, ngy - 1)), 2),
    )

    def face_copy(turn, side, src, dst):
        return pltpu.make_async_remote_copy(
            src_ref=src,
            dst_ref=dst.at[sides[side][2]],
            send_sem=ssem.at[turn * 4 + side],
            recv_sem=rsem.at[turn * 4 + sides[side][2]],
            device_id=sides[side][1],
            device_id_type=MESH,
        )

    def face_wait(turn, side, src, dst):
        return pltpu.make_async_remote_copy(
            src_ref=src,
            dst_ref=dst.at[side],
            send_sem=ssem.at[turn * 4 + side],
            recv_sem=rsem.at[turn * 4 + side],
            device_id=sides[side][1],
            device_id_type=MESH,
        )

    corners = []
    for a in (0, 1):
        for b in (0, 1):
            okay = jnp.logical_and(sides[a][0], sides[2 + b][0])
            corners.append((okay, (sides[a][1][0], sides[2 + b][1][1])))

    def corner_copy(index):
        return pltpu.make_async_remote_copy(
            src_ref=csend.at[index],
            dst_ref=crecv.at[3 - index],
            send_sem=cssem.at[index],
            recv_sem=crsem.at[3 - index],
            device_id=corners[index][1],
            device_id_type=MESH,
        )

    def corner_wait(index):
        return pltpu.make_async_remote_copy(
            src_ref=csend.at[index],
            dst_ref=crecv.at[index],
            send_sem=cssem.at[index],
            recv_sem=crsem.at[index],
            device_id=corners[index][1],
            device_id_type=MESH,
        )

    for side in range(4):
        @pl.when(jnp.logical_not(sides[side][0]))
        def _(side=side):
            recv1[side] = jnp.zeros(recv1.shape[1:], f32)
            for turn in range(2):
                recv23[turn, side] = jnp.zeros(recv23.shape[2:], f32)
    for index in range(4):
        @pl.when(jnp.logical_not(corners[index][0]))
        def _(index=index):
            crecv[index] = jnp.zeros(crecv.shape[1:], f32)

    def clear(ix, carry):
        base = pl.multiple_of(ix * step, 8)
        for y in (y0, y1, y2):
            y[:, pl.ds(base, EDGE), :] = jnp.zeros((3, EDGE, LANES), f32)
            y[:, pl.ds(base + EDGE + cy, EDGE), :] = jnp.zeros((3, EDGE, LANES), f32)
        cpad[pl.ds(base + step, EDGE), :] = jnp.zeros((EDGE, LANES), f32)
        cpad[pl.ds(base + step + EDGE + cy, EDGE), :] = jnp.zeros((EDGE, LANES), f32)
        return carry

    lax.fori_loop(0, cx + 2, clear, 0)
    for y in (y0, y1, y2):
        y[:, pl.ds(EDGE, cy), :] = jnp.zeros((3, cy, LANES), f32)
        y[:, pl.ds((cx + 1) * step + EDGE, cy), :] = jnp.zeros((3, cy, LANES), f32)
    for layer in (0, 1, cx + 2, cx + 3):
        cpad[pl.ds(layer * step + EDGE, cy), :] = jnp.zeros((cy, LANES), f32)

    load_c.wait()
    load_v.wait()
    last = (cx - 1) * cy
    for k in range(3):
        send1[0, k] = vol[k, 0:cy]
        send1[1, k] = vol[k, last:last + cy]
        send1[2, k] = vol[k, pl.ds(0, cx, stride=cy)]
        send1[3, k] = vol[k, pl.ds(cy - 1, cx, stride=cy)]
    for deep in range(2):
        send1[0, 3 + deep] = cin[deep * cy:(deep + 1) * cy]
        send1[1, 3 + deep] = cin[last - deep * cy:last - deep * cy + cy]
        send1[2, 3 + deep] = cin[pl.ds(deep, cx, stride=cy)]
        send1[3, 3 + deep] = cin[pl.ds(cy - 1 - deep, cx, stride=cy)]
    for index in range(4):
        row = (index // 2) * last + (index % 2) * (cy - 1)
        csend[index] = jnp.broadcast_to(cin[row:row + 1], (8, LANES))

    pl.semaphore_wait(barrier, n - 1)
    for side in range(4):
        @pl.when(sides[side][0])
        def _(side=side):
            face_copy(0, side, send1.at[side], recv1).start()
    for index in range(4):
        @pl.when(corners[index][0])
        def _(index=index):
            corner_copy(index).start()

    def all_copy(src, dst, sems, other, landing):
        return pltpu.make_async_remote_copy(
            src_ref=src.at[other],
            dst_ref=dst.at[landing],
            send_sem=sems[0].at[other],
            recv_sem=sems[1].at[landing],
            device_id=(other // ngy, lax.rem(other, ngy)),
            device_id_type=MESH,
        )

    def send_all(src, dst, sems):
        def go(i, carry):
            all_copy(src, dst, sems, lax.rem(me + i, n), me).start()
            return carry

        lax.fori_loop(1, n, go, 0)
        dst[me] = src[me]

    def take_all(src, dst, sems):
        def go(i, carry):
            other = lax.rem(me + i, n)
            all_copy(src, dst, sems, other, other).wait_recv()
            return carry

        lax.fori_loop(1, n, go, 0)

    def sent_all(src, dst, sems):
        def go(i, carry):
            all_copy(src, dst, sems, lax.rem(me + i, n), me).wait_send()
            return carry

        lax.fori_loop(1, n, go, 0)

    meta = (meta_send, meta_recv, (mssem, mrsem))
    surf = (surf_send, surf_recv, (ussem, ursem))

    def fill(ix, carry):
        to = pl.multiple_of((ix + 2) * step + EDGE, 8)
        cpad[pl.ds(to, cy), :] = cin[pl.ds(pl.multiple_of(ix * cy, 8), cy), :] * (OMEGA / 2)
        return carry

    lax.fori_loop(0, cx, fill, 0, unroll=UNROLL)
    def inverse(center, others):
        lane = lax.broadcasted_iota(jnp.int32, center.shape, 1)
        above = jnp.where(lane == LANES - 1, 0.0, pltpu.roll(center, LANES - 1, 1))
        below = jnp.where(lane == 0, 0.0, pltpu.roll(center, 1, 1))
        total = 6.0 * center + above + below
        for other in others:
            total = total + other
        return OMEGA / total, above

    def scale(it, carry):
        done = []
        for u in range(UNROLL):
            ix = it * UNROLL + u
            at = pl.multiple_of((ix + 2) * step + EDGE, 8)
            to = pl.multiple_of(ix * cy, 8)
            center = cpad[pl.ds(at, cy), :]
            inv, above = inverse(
                center,
                [cpad[pl.ds(at + d, cy), :] for d in (-step, step, -1, 1)],
            )
            lane = lax.broadcasted_iota(jnp.int32, center.shape, 1)
            up = jnp.where(lane == LANES - 1, 0.0, center + above)
            done.append((at, to, inv, up, vol[:, pl.ds(to, cy), :] * inv[None]))
        for at, to, inv, up, scaled in done:
            rd[pl.ds(to, cy), :] = inv
            wz[pl.ds(to, cy), :] = up
            y0[:, pl.ds(pl.multiple_of(at - step, 8), cy), :] = scaled
        return carry

    lax.fori_loop(0, cx // UNROLL, scale, 0)

    def sweep(vsrc, vdst, ysrc, ydst):
        def layers(it, carry):
            done = []
            for u in range(UNROLL):
                ix = it * UNROLL + u
                at = pl.multiple_of((ix + 1) * step + EDGE, 8)
                ct = pl.multiple_of((ix + 2) * step + EDGE, 8)
                to = pl.multiple_of(ix * cy, 8)
                center = cpad[pl.ds(ct, cy), :]
                up = wz[pl.ds(to, cy), :][None]
                mid = ysrc[:, pl.ds(at, cy), :]
                total = up * pltpu.roll(mid, LANES - 1, 2) + pltpu.roll(up * mid, 1, 2)
                for d in (step, -step, 1, -1):
                    weight = center + cpad[pl.ds(ct + d, cy), :]
                    total = total + weight[None] * ysrc[:, pl.ds(at + d, cy), :]
                new = vol[:, pl.ds(to, cy), :] + (1.0 - OMEGA) * vsrc[:, pl.ds(to, cy), :] + total
                done.append((at, to, new))
            for at, to, new in done:
                vdst[:, pl.ds(to, cy), :] = new
                if ydst is not None:
                    ydst[:, pl.ds(at, cy), :] = new * rd[pl.ds(to, cy), :][None]
            return carry

        lax.fori_loop(0, cx // UNROLL, layers, 0)

    def send_faces(turn, y):
        low, high = step + EDGE, cx * step + EDGE
        for k in range(3):
            send_y[turn - 1, 2, k] = y[k, pl.ds(low, cx, stride=step), :]
            send_y[turn - 1, 3, k] = y[k, pl.ds(low + cy - 1, cx, stride=step), :]
            send_y[turn - 1, 0, k] = y[k, low:low + cy, :]
            send_y[turn - 1, 1, k] = y[k, high:high + cy, :]
        for side in range(4):
            @pl.when(sides[side][0])
            def _(side=side):
                face_copy(turn, side, send_y.at[turn - 1, side], recv23.at[turn - 1]).start()

    def add_faces(turn, val, ydst):
        for side in range(4):
            @pl.when(sides[side][0])
            def _(side=side):
                face_wait(turn, side, send_y.at[turn - 1, side], recv23.at[turn - 1]).wait_recv()
        for side in range(4):
            if side < 2:
                ct = (2 + side * (cx - 1)) * step + EDGE
                to = side * last
                outer = ct + (step if side else -step)
                here, there, flat = pl.ds(ct, cy), pl.ds(outer, cy), pl.ds(to, cy)
                pad = pl.ds(ct - step, cy)
            else:
                shift = (side - 2) * (cy - 1)
                ct = 2 * step + EDGE + shift
                outer = ct + (1 if side == 3 else -1)
                here, there = pl.ds(ct, cx, stride=step), pl.ds(outer, cx, stride=step)
                flat = pl.ds(shift, cx, stride=cy)
                pad = pl.ds(ct - step, cx, stride=step)
            weight = cpad[here, :] + cpad[there, :]
            inv = rd[flat, :]
            for k in range(3):
                more = weight * recv23[turn - 1, side, k]
                val[k, flat, :] = val[k, flat, :] + more
                if ydst is not None:
                    ydst[k, pad, :] = ydst[k, pad, :] + more * inv

    def line(kind, j, height):
        if kind == 0:
            base = (j + height) * step + EDGE
            return lambda d: pl.ds(base + d, cy)
        base = height * step + EDGE + j
        return lambda d: pl.ds(base + d, cx, stride=step)

    def flat_line(kind, j):
        return pl.ds(j * cy, cy) if kind == 0 else pl.ds(j, cx, stride=cy)

    def scale_line(kind, j):
        c, flat, yl = line(kind, j, 2), flat_line(kind, j), line(kind, j, 1)
        inv, _ = inverse(cpad[c(0), :], [cpad[c(d), :] for d in (-step, step, -1, 1)])
        rd[flat, :] = inv
        for k in range(3):
            y0[k, yl(0), :] = vol[k, flat, :] * inv

    def sweep_line(kind, j):
        c, flat, yl = line(kind, j, 2), flat_line(kind, j), line(kind, j, 1)
        center, up, inv = cpad[c(0), :], wz[flat, :], rd[flat, :]
        weights = [(d, center + cpad[c(d), :]) for d in (step, -step, 1, -1)]
        done = []
        for k in range(3):
            mid, first = y0[k, yl(0), :], vol[k, flat, :]
            total = up * pltpu.roll(mid, LANES - 1, 1) + pltpu.roll(up * mid, 1, 1)
            for d, weight in weights:
                total = total + weight * y0[k, yl(d), :]
            done.append(first + (1.0 - OMEGA) * first + total)
        for k in range(3):
            field[k, flat, :] = done[k]
            y1[k, yl(0), :] = done[k] * inv

    sweep(vol, field, y0, y1)
    for side in range(4):
        @pl.when(sides[side][0])
        def _(side=side):
            face_wait(0, side, send1.at[side], recv1).wait_recv()
    for index in range(4):
        @pl.when(corners[index][0])
        def _(index=index):
            corner_wait(index).wait_recv()
    half = OMEGA / 2
    for deep in range(2):
        low, high = (1 - deep) * step + EDGE, (cx + 2 + deep) * step + EDGE
        cpad[low:low + cy, :] = recv1[0, 3 + deep] * half
        cpad[high:high + cy, :] = recv1[1, 3 + deep] * half
        cpad[pl.ds(2 * step + EDGE - 1 - deep, cx, stride=step), :] = recv1[2, 3 + deep] * half
        cpad[pl.ds(2 * step + EDGE + cy + deep, cx, stride=step), :] = recv1[3, 3 + deep] * half
    for index in range(4):
        row = (1 + (index // 2) * (cx + 1)) * step + EDGE - 1 + (index % 2) * (cy + 1)
        cpad[row:row + 1, :] = crecv[index, 0:1] * half

    ends = ((0, 0), (0, cx - 1), (1, 0), (1, cy - 1))
    beside = ((0, 1), (0, cx - 2), (1, 1), (1, cy - 2))
    for kind, j in ends:
        scale_line(kind, j)
    for side in range(4):
        if side < 2:
            at = (1 + side * (cx + 1)) * step + EDGE
            inv, _ = inverse(
                cpad[at:at + cy, :],
                [cpad[at + d:at + d + cy, :] for d in (-step, step, -1, 1)],
            )
            for k in range(3):
                y0[k, at - step:at - step + cy, :] = recv1[side, k] * inv
        else:
            at = 2 * step + EDGE - 1 + (side - 2) * (cy + 1)
            inv, _ = inverse(
                cpad[pl.ds(at, cx, stride=step), :],
                [cpad[pl.ds(at + d, cx, stride=step), :] for d in (-step, step, -1, 1)],
            )
            for k in range(3):
                y0[k, pl.ds(at - step, cx, stride=step), :] = recv1[side, k] * inv

    for kind, j in ends:
        sweep_line(kind, j)
    send_faces(1, y1)
    for kind, j in beside:
        sweep_line(kind, j)
    sweep(field, val, y1, y2)
    patch = patch_ref[...]
    hot = (lax.broadcasted_iota(jnp.int32, (n, rows), 0) == patch).astype(f32)
    hot_ref[...] = hot
    upper = (
        lax.broadcasted_iota(jnp.int32, (LANES, LANES), 0)
        <= lax.broadcasted_iota(jnp.int32, (LANES, LANES), 1)
    ).astype(f32).astype(bf16)
    before = jnp.zeros((n, 1), f32)
    for chunk in range(rows // LANES):
        part = hot[:, chunk * LANES:(chunk + 1) * LANES]
        count = jnp.dot(part.astype(bf16), upper, preferred_element_type=f32)
        rank = jnp.sum(part * (count + before), axis=0, keepdims=True) - 1.0
        before = before + count[:, LANES - 1:LANES]
        place = lax.broadcasted_iota(jnp.int32, (LANES, LANES), 0)
        slot_ref[:, chunk * LANES:(chunk + 1) * LANES] = (
            (place == rank.astype(jnp.int32)).astype(f32).astype(bf16)
        )
    add_faces(1, val, y2)
    send_faces(2, y2)
    sweep(val, field, y2, None)
    hot16 = hot_ref[...].astype(bf16)
    slots = slot_ref[...]
    stack = []
    for q in range(2):
        stack += split(param_ref[q:q + 1, :], 3)
    for q in range(2):
        stack.append(span_ref[q:q + 1, :].astype(f32).astype(bf16))
    out = nt_dot(jnp.concatenate([hot16 * part for part in stack], axis=0), slots)
    out = [out[i * n:(i + 1) * n] for i in range(8)]
    meta_send[:, 0, :] = out[0] + out[1] + out[2]
    meta_send[:, 1, :] = out[3] + out[4] + out[5]
    meta_send[:, 2, :] = out[6]
    meta_send[:, 3, :] = out[7]
    send_all(*meta)
    add_faces(2, field, None)


    def surface(ix, carry):
        to = pl.ds(pl.multiple_of(ix * cy, 8), cy)
        lane = lax.broadcasted_iota(jnp.int32, (cy, LANES), 1)
        inv = rd[to, :] * OMEGA
        out = jnp.where(lane == 0, field[0, to, :] * inv, 0.0)
        for k in (1, 2):
            out = jnp.where(lane == k, pltpu.roll(field[k, to, :] * inv, k, 1), out)
        xcol[to, :] = out
        return carry

    lax.fori_loop(0, cx, surface, 0, unroll=UNROLL)
    surf_rows = jnp.concatenate(
        [xcol[c * LANES:(c + 1) * LANES, :].T[0:8] for c in range(rows // LANES)], axis=1
    )
    hot16 = hot_ref[...].astype(bf16)
    slots = slot_ref[...]
    stack = []
    for k in range(3):
        stack += split(surf_rows[k:k + 1, :], 3)
    out = nt_dot(jnp.concatenate([hot16 * part for part in stack], axis=0), slots)
    out = [out[i * n:(i + 1) * n] for i in range(9)]
    for k in range(3):
        surf_send[:, k, :] = out[3 * k] + out[3 * k + 1] + out[3 * k + 2]
    surf_send[:, 3, :] = jnp.zeros((n, LANES), f32)
    send_all(*surf)

    take_all(*meta)
    basis_u = pieces(meta_recv[:, 0, :])
    basis_v = pieces(meta_recv[:, 1, :])
    span_u = meta_recv[:, 2, :].astype(jnp.int32)
    span_v = meta_recv[:, 3, :].astype(jnp.int32)
    knot = lax.broadcasted_iota(jnp.int32, (NC, LANES), 0)

    def spline(span, basis, d):
        offset = knot - span[d:d + 1, :]
        out = jnp.where(offset == 0, basis[0][d:d + 1, :], 0.0)
        for index in range(1, 4):
            out = jnp.where(offset == index, basis[index][d:d + 1, :], out)
        return out

    for d in range(n):
        lanes = slice(d * LANES, (d + 1) * LANES)
        bu_ref[:, lanes] = spline(span_u, basis_u, d)
        high, low = split(spline(span_v, basis_v, d), 2)
        bv_ref[:NC, lanes] = high
        bv_ref[NC:, lanes] = low

    take_all(*surf)

    for side in range(4):
        @pl.when(sides[side][0])
        def _(side=side):
            face_copy(0, side, send1.at[side], recv1).wait_send()
            for turn in (1, 2):
                face_copy(turn, side, send_y.at[turn - 1, side], recv23.at[turn - 1]).wait_send()
    for index in range(4):
        @pl.when(corners[index][0])
        def _(index=index):
            corner_copy(index).wait_send()
    sent_all(*meta)
    sent_all(*surf)


def product(n, val, surf_ref, bu_ref, bv_ref, field, grad_ref, sem):
    store = pltpu.make_async_copy(val, field, sem)
    store.start()
    group = 8
    total = jnp.zeros((6 * NC, 2 * NC), jnp.float32)
    for first in range(0, n, group):
        lanes = slice(first * LANES, (first + group) * LANES)
        bu = bu_ref[:, lanes]
        left = jnp.concatenate(
            [
                bu * jnp.concatenate(
                    [surf_ref[d, k:k + 1, :] for d in range(first, first + group)],
                    axis=1,
                )
                for k in range(3)
            ],
            axis=0,
        )
        total = total + nt_dot(jnp.concatenate(split(left, 2), axis=0), bv_ref[:, lanes])
    for k in range(3):
        high, low = total[k * NC:(k + 1) * NC], total[(3 + k) * NC:(4 + k) * NC]
        grad_ref[k] = high[:, :NC] + high[:, NC:] + low[:, :NC] + low[:, NC:]
    store.wait()


def body(volume_sens, stiffness, patch_of_row, knot_spans, span_params):
    ngx, ngy = lax.axis_size("gx"), lax.axis_size("gy")
    n = ngx * ngy
    _, cx, cy, nz = volume_sens.shape
    rows = cx * cy
    step = cy + 2 * EDGE
    f32, bf16 = jnp.float32, jnp.bfloat16
    dma = pltpu.SemaphoreType.DMA
    vmem = pl.BlockSpec(memory_space=pltpu.VMEM)
    room = 62 * 2**20 - 4 * (3 * rows * nz + n * 4 * LANES + 2 * NC * n * LANES)
    found = pl.pallas_call(
        functools.partial(kernel, (ngx, ngy, cx, cy, rows)),
        out_shape=(
            pltpu.VMEM((3, rows, nz), f32),
            pltpu.VMEM((n, 4, LANES), f32),
            pltpu.VMEM((NC, n * LANES), f32),
            pltpu.VMEM((2 * NC, n * LANES), bf16),
        ),
        in_specs=[
            pl.BlockSpec(memory_space=pl.ANY),
            pl.BlockSpec(memory_space=pl.ANY),
            pl.BlockSpec(memory_space=pltpu.VMEM),
            pl.BlockSpec(memory_space=pltpu.VMEM),
            pl.BlockSpec(memory_space=pltpu.VMEM),
        ],
        out_specs=(vmem,) * 4,
        scratch_shapes=[
            pltpu.VMEM((3, rows, nz), f32),
            pltpu.VMEM((rows, nz), f32),
            pltpu.VMEM(((cx + 4) * step, nz), f32),
            pltpu.VMEM((rows, nz), f32),
            pltpu.VMEM((rows, nz), f32),
            pltpu.VMEM((3, rows, nz), f32),
            pltpu.VMEM((3, (cx + 2) * step, nz), f32),
            pltpu.VMEM((3, (cx + 2) * step, nz), f32),
            pltpu.VMEM((3, (cx + 2) * step, nz), f32),
            pltpu.VMEM((4, 5, cy, nz), f32),
            pltpu.VMEM((4, 5, cy, nz), f32),
            pltpu.VMEM((4, 8, nz), f32),
            pltpu.VMEM((4, 8, nz), f32),
            pltpu.VMEM((2, 4, 3, cy, nz), f32),
            pltpu.VMEM((2, 4, 3, cy, nz), f32),
            pltpu.VMEM((n, rows), f32),
            pltpu.VMEM((LANES, rows), bf16),
            pltpu.VMEM((rows, nz), f32),
            pltpu.VMEM((n, 4, LANES), f32),
            pltpu.VMEM((n, 4, LANES), f32),
            pltpu.VMEM((n, 4, LANES), f32),
            dma((2,)),
            dma((12,)),
            dma((12,)),
            dma((4,)),
            dma((4,)),
            dma((n,)),
            dma((n,)),
            dma((n,)),
            dma((n,)),
        ],
        compiler_params=pltpu.CompilerParams(
            collective_id=0, has_side_effects=True, vmem_limit_bytes=room
        ),
    )(
        volume_sens.reshape(3, rows, nz),
        stiffness.reshape(rows, nz),
        patch_of_row.reshape(1, rows),
        knot_spans[0].T,
        span_params[0].T,
    )
    field, grads = pl.pallas_call(
        functools.partial(product, n),
        out_shape=(
            jax.ShapeDtypeStruct((3, rows, nz), f32),
            jax.ShapeDtypeStruct((3, NC, NC), f32),
        ),
        in_specs=[vmem] * 4,
        out_specs=(pl.BlockSpec(memory_space=pl.ANY), vmem),
        scratch_shapes=[dma],
        compiler_params=pltpu.CompilerParams(vmem_limit_bytes=32 * 2**20),
    )(*found)
    return field.reshape(volume_sens.shape), grads[None]


def solution(mesh):
    placed = (
        P(None, "gx", "gy", None),
        P("gx", "gy", None),
        P(("gx", "gy"), None, None),
        P(("gx", "gy"), None, None),
        P(("gx", "gy"), None, None),
    )
    return jax.shard_map(
        body,
        mesh=mesh,
        in_specs=placed,
        out_specs=(P(None, "gx", "gy", None), P(("gx", "gy"), None, None, None)),
        check_vma=False,
    )
```

```python
import functools

import jax
import jax.numpy as jnp
from jax import lax
from jax.experimental import pallas as pl
from jax.experimental.pallas import tpu as pltpu
from jax.sharding import PartitionSpec as P

SWEEPS = 3
NC = 64
OMEGA = 2.0 / 3.0
LANES = 128
EDGE = 8
UNROLL = 4
MESH = pl.DeviceIdType.MESH
NT = (((1,), (1,)), ((), ()))


def pieces(param):
    other = 1.0 - param
    square = param * param
    cube = square * param
    return [
        other * other * other / 6.0,
        (3.0 * cube - 6.0 * square + 4.0) / 6.0,
        (-3.0 * cube + 3.0 * square + 3.0 * param + 1.0) / 6.0,
        cube / 6.0,
    ]


def split(values, count):
    parts = []
    for _ in range(count):
        part = values.astype(jnp.bfloat16)
        parts.append(part)
        values = values - part.astype(jnp.float32)
    return parts


def nt_dot(left, right):
    return lax.dot_general(left, right, NT, preferred_element_type=jnp.float32)


def kernel(
    sizes,
    vol_hbm, stiff_hbm, patch_ref, span_ref, param_ref,
    field, surf_recv, bu_ref, bv_ref,
    vol, cin, cpad, rd, wz, val, y0, y1, y2,
    send1, recv1, csend, crecv, send_y, recv23,
    hot_ref, slot_ref, xcol, face_w, face_i, hot_face, slot_face,
    meta_send, meta_recv, surf_send,
    in_sem, ssem, rsem, cssem, crsem, mssem, mrsem, ussem, ursem,
):
    ngx, ngy, cx, cy, rows = sizes
    n = ngx * ngy
    step = cy + 2 * EDGE
    gx, gy = lax.axis_index("gx"), lax.axis_index("gy")
    me = gx * ngy + gy
    f32, bf16 = jnp.float32, jnp.bfloat16

    load_c = pltpu.make_async_copy(stiff_hbm, cin, in_sem.at[0])
    load_v = [pltpu.make_async_copy(vol_hbm.at[k], vol.at[k], in_sem.at[1 + k]) for k in range(3)]
    load_c.start()
    for k in range(3):
        load_v[k].start()

    barrier = pltpu.get_barrier_semaphore()

    def greet(i, carry):
        to = lax.rem(me + i, n)
        pl.semaphore_signal(barrier, inc=1, device_id=(to // ngy, lax.rem(to, ngy)), device_id_type=MESH)
        return carry

    lax.fori_loop(1, n, greet, 0)

    sides = (
        (gx > 0, (jnp.maximum(gx - 1, 0), gy), 1),
        (gx < ngx - 1, (jnp.minimum(gx + 1, ngx - 1), gy), 0),
        (gy > 0, (gx, jnp.maximum(gy - 1, 0)), 3),
        (gy < ngy - 1, (gx, jnp.minimum(gy + 1, ngy - 1)), 2),
    )

    def face_copy(turn, side, src, dst):
        return pltpu.make_async_remote_copy(
            src_ref=src,
            dst_ref=dst.at[sides[side][2]],
            send_sem=ssem.at[turn * 4 + side],
            recv_sem=rsem.at[turn * 4 + sides[side][2]],
            device_id=sides[side][1],
            device_id_type=MESH,
        )

    def face_wait(turn, side, src, dst):
        return pltpu.make_async_remote_copy(
            src_ref=src,
            dst_ref=dst.at[side],
            send_sem=ssem.at[turn * 4 + side],
            recv_sem=rsem.at[turn * 4 + side],
            device_id=sides[side][1],
            device_id_type=MESH,
        )

    corners = []
    for a in (0, 1):
        for b in (0, 1):
            okay = jnp.logical_and(sides[a][0], sides[2 + b][0])
            corners.append((okay, (sides[a][1][0], sides[2 + b][1][1])))

    def corner_copy(index):
        return pltpu.make_async_remote_copy(
            src_ref=csend.at[index],
            dst_ref=crecv.at[3 - index],
            send_sem=cssem.at[index],
            recv_sem=crsem.at[3 - index],
            device_id=corners[index][1],
            device_id_type=MESH,
        )

    def corner_wait(index):
        return pltpu.make_async_remote_copy(
            src_ref=csend.at[index],
            dst_ref=crecv.at[index],
            send_sem=cssem.at[index],
            recv_sem=crsem.at[index],
            device_id=corners[index][1],
            device_id_type=MESH,
        )

    for side in range(4):
        @pl.when(jnp.logical_not(sides[side][0]))
        def _(side=side):
            recv1[side] = jnp.zeros(recv1.shape[1:], f32)
            for turn in range(2):
                recv23[turn, side] = jnp.zeros(recv23.shape[2:], f32)
    for index in range(4):
        @pl.when(jnp.logical_not(corners[index][0]))
        def _(index=index):
            crecv[index] = jnp.zeros(crecv.shape[1:], f32)

    def clear(ix, carry):
        base = pl.multiple_of(ix * step, 8)
        for y in (y0, y1, y2):
            y[:, pl.ds(base, EDGE), :] = jnp.zeros((3, EDGE, LANES), f32)
            y[:, pl.ds(base + EDGE + cy, EDGE), :] = jnp.zeros((3, EDGE, LANES), f32)
        cpad[pl.ds(base + step, EDGE), :] = jnp.zeros((EDGE, LANES), f32)
        cpad[pl.ds(base + step + EDGE + cy, EDGE), :] = jnp.zeros((EDGE, LANES), f32)
        return carry

    lax.fori_loop(0, cx + 2, clear, 0)
    for y in (y0, y1, y2):
        y[:, pl.ds(EDGE, cy), :] = jnp.zeros((3, cy, LANES), f32)
        y[:, pl.ds((cx + 1) * step + EDGE, cy), :] = jnp.zeros((3, cy, LANES), f32)
    for layer in (0, 1, cx + 2, cx + 3):
        cpad[pl.ds(layer * step + EDGE, cy), :] = jnp.zeros((cy, LANES), f32)

    load_c.wait()
    last = (cx - 1) * cy
    for deep in range(2):
        send1[0, 3 + deep] = cin[deep * cy:(deep + 1) * cy]
        send1[1, 3 + deep] = cin[last - deep * cy:last - deep * cy + cy]
        send1[2, 3 + deep] = cin[pl.ds(deep, cx, stride=cy)]
        send1[3, 3 + deep] = cin[pl.ds(cy - 1 - deep, cx, stride=cy)]
    for index in range(4):
        row = (index // 2) * last + (index % 2) * (cy - 1)
        csend[index] = jnp.broadcast_to(cin[row:row + 1], (8, LANES))

    for k in range(3):
        load_v[k].wait()
        send1[0, k] = vol[k, 0:cy]
        send1[1, k] = vol[k, last:last + cy]
        send1[2, k] = vol[k, pl.ds(0, cx, stride=cy)]
        send1[3, k] = vol[k, pl.ds(cy - 1, cx, stride=cy)]

    pl.semaphore_wait(barrier, n - 1)
    for side in (2, 3, 0, 1):
        @pl.when(sides[side][0])
        def _(side=side):
            face_copy(0, side, send1.at[side], recv1).start()
    for index in range(4):
        @pl.when(corners[index][0])
        def _(index=index):
            corner_copy(index).start()

    def all_copy(src, dst, sems, other, landing):
        return pltpu.make_async_remote_copy(
            src_ref=src.at[other],
            dst_ref=dst.at[landing],
            send_sem=sems[0],
            recv_sem=sems[1],
            device_id=(other // ngy, lax.rem(other, ngy)),
            device_id_type=MESH,
        )

    def send_all(src, dst, sems):
        def go(i, carry):
            all_copy(src, dst, sems, lax.rem(me + i, n), me).start()
            return carry

        lax.fori_loop(1, n, go, 0)
        dst[me] = src[me]

    def every(src, dst, sems):
        other = lax.rem(me + 1, n)
        return pltpu.make_async_remote_copy(
            src_ref=src.at[pl.ds(0, n - 1)],
            dst_ref=dst.at[pl.ds(0, n - 1)],
            send_sem=sems[0],
            recv_sem=sems[1],
            device_id=(other // ngy, lax.rem(other, ngy)),
            device_id_type=MESH,
        )

    meta = (meta_send, meta_recv, (mssem, mrsem))
    surf = (surf_send, surf_recv, (ussem, ursem))

    def fill(ix, carry):
        to = pl.multiple_of((ix + 2) * step + EDGE, 8)
        cpad[pl.ds(to, cy), :] = cin[pl.ds(pl.multiple_of(ix * cy, 8), cy), :] * (OMEGA / 2)
        return carry

    lax.fori_loop(0, cx, fill, 0, unroll=UNROLL)
    def inverse(center, others):
        lane = lax.broadcasted_iota(jnp.int32, center.shape, 1)
        above = jnp.where(lane == LANES - 1, 0.0, pltpu.roll(center, LANES - 1, 1))
        below = jnp.where(lane == 0, 0.0, pltpu.roll(center, 1, 1))
        total = 6.0 * center + above + below
        for other in others:
            total = total + other
        return OMEGA / total, above

    def scale(it, carry):
        done = []
        for u in range(UNROLL):
            ix = it * UNROLL + u
            at = pl.multiple_of((ix + 2) * step + EDGE, 8)
            to = pl.multiple_of(ix * cy, 8)
            center = cpad[pl.ds(at, cy), :]
            inv, above = inverse(
                center,
                [cpad[pl.ds(at + d, cy), :] for d in (-step, step, -1, 1)],
            )
            lane = lax.broadcasted_iota(jnp.int32, center.shape, 1)
            up = jnp.where(lane == LANES - 1, 0.0, center + above)
            done.append((at, to, inv, up, vol[:, pl.ds(to, cy), :] * inv[None]))
        for at, to, inv, up, scaled in done:
            rd[pl.ds(to, cy), :] = inv
            wz[pl.ds(to, cy), :] = up
            y0[:, pl.ds(pl.multiple_of(at - step, 8), cy), :] = scaled
        return carry

    lax.fori_loop(0, cx // UNROLL, scale, 0)

    def sweep(vsrc, vdst, ysrc, ydst):
        def layers(it, carry):
            done = []
            for u in range(UNROLL):
                ix = it * UNROLL + u
                at = pl.multiple_of((ix + 1) * step + EDGE, 8)
                ct = pl.multiple_of((ix + 2) * step + EDGE, 8)
                to = pl.multiple_of(ix * cy, 8)
                center = cpad[pl.ds(ct, cy), :]
                up = wz[pl.ds(to, cy), :][None]
                mid = ysrc[:, pl.ds(at, cy), :]
                total = up * pltpu.roll(mid, LANES - 1, 2) + pltpu.roll(up * mid, 1, 2)
                for d in (step, -step, 1, -1):
                    weight = center + cpad[pl.ds(ct + d, cy), :]
                    total = total + weight[None] * ysrc[:, pl.ds(at + d, cy), :]
                new = vol[:, pl.ds(to, cy), :] + (1.0 - OMEGA) * vsrc[:, pl.ds(to, cy), :] + total
                done.append((at, to, new))
            for at, to, new in done:
                vdst[:, pl.ds(to, cy), :] = new
                if ydst is not None:
                    ydst[:, pl.ds(at, cy), :] = new * rd[pl.ds(to, cy), :][None]
            return carry

        lax.fori_loop(0, cx // UNROLL, layers, 0)

    def line(kind, j, height):
        if kind == 0:
            base = (j + height) * step + EDGE
            return lambda d: pl.ds(base + d, cy)
        base = height * step + EDGE + j
        return lambda d: pl.ds(base + d, cx, stride=step)

    def flat_line(kind, j):
        return pl.ds(j * cy, cy) if kind == 0 else pl.ds(j, cx, stride=cy)

    def scale_line(kind, j):
        c, flat, yl = line(kind, j, 2), flat_line(kind, j), line(kind, j, 1)
        inv, _ = inverse(cpad[c(0), :], [cpad[c(d), :] for d in (-step, step, -1, 1)])
        rd[flat, :] = inv
        for k in range(3):
            y0[k, yl(0), :] = vol[k, flat, :] * inv

    def sweep_line(kind, j, side=None):
        c, flat, yl = line(kind, j, 2), flat_line(kind, j), line(kind, j, 1)
        center, up, inv = cpad[c(0), :], wz[flat, :], rd[flat, :]
        weights = [(d, center + cpad[c(d), :]) for d in (step, -step, 1, -1)]
        done = []
        for k in range(3):
            mid, first = y0[k, yl(0), :], vol[k, flat, :]
            total = up * pltpu.roll(mid, LANES - 1, 1) + pltpu.roll(up * mid, 1, 1)
            for d, weight in weights:
                total = total + weight * y0[k, yl(d), :]
            done.append(first + (1.0 - OMEGA) * first + total)
        for k in range(3):
            field[k, flat, :] = done[k]
            y1[k, yl(0), :] = done[k] * inv
            if side is not None:
                send_y[0, side, k] = done[k] * inv
        if side is not None:
            send_face(1, side)

    def send_face(turn, side):
        @pl.when(sides[side][0])
        def _():
            face_copy(turn, side, send_y.at[turn - 1, side], recv23.at[turn - 1]).start()

    def take_face(turn, side):
        @pl.when(sides[side][0])
        def _():
            face_wait(turn, side, send_y.at[turn - 1, side], recv23.at[turn - 1]).wait_recv()

    ends = ((0, 0), (0, cx - 1), (1, 0), (1, cy - 1))
    beside = ((0, 1), (0, cx - 2), (1, 1), (1, cy - 2))

    def add_values(turn, dst):
        for side in range(4):
            flat = flat_line(*ends[side])
            for k in range(3):
                dst[k, flat, :] = dst[k, flat, :] + face_w[side] * recv23[turn - 1, side, k]

    sweep(vol, field, y0, y1)
    for side in range(4):
        @pl.when(sides[side][0])
        def _(side=side):
            face_wait(0, side, send1.at[side], recv1).wait_recv()
    for index in range(4):
        @pl.when(corners[index][0])
        def _(index=index):
            corner_wait(index).wait_recv()
    half = OMEGA / 2
    for deep in range(2):
        low, high = (1 - deep) * step + EDGE, (cx + 2 + deep) * step + EDGE
        cpad[low:low + cy, :] = recv1[0, 3 + deep] * half
        cpad[high:high + cy, :] = recv1[1, 3 + deep] * half
        cpad[pl.ds(2 * step + EDGE - 1 - deep, cx, stride=step), :] = recv1[2, 3 + deep] * half
        cpad[pl.ds(2 * step + EDGE + cy + deep, cx, stride=step), :] = recv1[3, 3 + deep] * half
    for index in range(4):
        row = (1 + (index // 2) * (cx + 1)) * step + EDGE - 1 + (index % 2) * (cy + 1)
        cpad[row:row + 1, :] = crecv[index, 0:1] * half

    for kind, j in ends:
        scale_line(kind, j)
    for side in range(4):
        if side < 2:
            at = (1 + side * (cx + 1)) * step + EDGE
            inv, _ = inverse(
                cpad[at:at + cy, :],
                [cpad[at + d:at + d + cy, :] for d in (-step, step, -1, 1)],
            )
            for k in range(3):
                y0[k, at - step:at - step + cy, :] = recv1[side, k] * inv
        else:
            at = 2 * step + EDGE - 1 + (side - 2) * (cy + 1)
            inv, _ = inverse(
                cpad[pl.ds(at, cx, stride=step), :],
                [cpad[pl.ds(at + d, cx, stride=step), :] for d in (-step, step, -1, 1)],
            )
            for k in range(3):
                y0[k, pl.ds(at - step, cx, stride=step), :] = recv1[side, k] * inv

    for side in (2, 3, 0, 1):
        sweep_line(*ends[side], side)
    for kind, j in beside:
        sweep_line(kind, j)
    for side, out in enumerate((-step, step, -1, 1)):
        at = line(*ends[side], 2)
        weight = cpad[at(0), :] + cpad[at(out), :]
        face_w[side] = weight
        face_i[side] = weight * rd[flat_line(*ends[side]), :]
    sweep(field, val, y1, y2)
    patch = patch_ref[...]
    hot = (lax.broadcasted_iota(jnp.int32, (n, rows), 0) == patch).astype(f32)
    hot_ref[...] = hot
    upper = (
        lax.broadcasted_iota(jnp.int32, (LANES, LANES), 0)
        <= lax.broadcasted_iota(jnp.int32, (LANES, LANES), 1)
    ).astype(f32).astype(bf16)
    before = jnp.zeros((n, 1), f32)
    for chunk in range(rows // LANES):
        part = hot[:, chunk * LANES:(chunk + 1) * LANES]
        count = jnp.dot(part.astype(bf16), upper, preferred_element_type=f32)
        rank = jnp.sum(part * (count + before), axis=0, keepdims=True) - 1.0
        before = before + count[:, LANES - 1:LANES]
        place = lax.broadcasted_iota(jnp.int32, (LANES, LANES), 0)
        slot_ref[:, chunk * LANES:(chunk + 1) * LANES] = (
            (place == rank.astype(jnp.int32)).astype(f32).astype(bf16)
        )
    face = lax.broadcasted_iota(jnp.int32, (rows, LANES), 1)
    part = face % cy
    where = jnp.where(face < cy, part, last + part)
    where = jnp.where(face >= 2 * cy, part * cy, where)
    where = jnp.where(face >= 3 * cy, part * cy + cy - 1, where)
    pick = (lax.broadcasted_iota(jnp.int32, (rows, LANES), 0) == where).astype(f32).astype(bf16)
    hot_face[...] = jnp.dot(hot.astype(bf16), pick, preferred_element_type=f32)
    slot_face[...] = jnp.dot(slot_ref[...], pick, preferred_element_type=f32).astype(bf16)

    for side in (0, 1, 2, 3):
        take_face(1, side)
        at = line(*ends[side], 1)(0)
        for k in range(3):
            new = y2[k, at, :] + face_i[side] * recv23[0, side, k]
            y2[k, at, :] = new
            if side > 1:
                send_y[1, side, k] = new
        if side > 1:
            send_face(2, side)
    for side in (0, 1):
        at = line(*ends[side], 1)(0)
        for k in range(3):
            send_y[1, side, k] = y2[k, at, :]
        send_face(2, side)
    add_values(1, val)
    sweep(val, field, y2, None)
    hot16 = hot_ref[...].astype(bf16)
    slots = slot_ref[...]
    stack = []
    for q in range(2):
        stack += split(param_ref[q:q + 1, :], 2)
    for q in range(2):
        stack.append(span_ref[q:q + 1, :].astype(f32).astype(bf16))
    out = nt_dot(jnp.concatenate([hot16 * part for part in stack], axis=0), slots)
    out = [out[i * n:(i + 1) * n] for i in range(6)]
    meta_send[:, 0, :] = out[0] + out[1]
    meta_send[:, 1, :] = out[2] + out[3]
    meta_send[:, 2, :] = out[4]
    meta_send[:, 3, :] = out[5]
    send_all(*meta)


    def surface(ix, carry):
        to = pl.ds(pl.multiple_of(ix * cy, 8), cy)
        lane = lax.broadcasted_iota(jnp.int32, (cy, LANES), 1)
        inv = rd[to, :] * OMEGA
        out = jnp.where(lane == 0, field[0, to, :] * inv, 0.0)
        for k in (1, 2):
            out = jnp.where(lane == k, pltpu.roll(field[k, to, :] * inv, k, 1), out)
        xcol[to, :] = out
        return carry

    lax.fori_loop(0, cx, surface, 0, unroll=UNROLL)
    surf_rows = jnp.concatenate(
        [xcol[c * LANES:(c + 1) * LANES, :].T[0:8] for c in range(rows // LANES)], axis=1
    )
    def route(values, hot16, slots):
        stack = []
        for k in range(3):
            stack += split(values[k:k + 1, :], 2)
        out = nt_dot(jnp.concatenate([hot16 * part for part in stack], axis=0), slots)
        return [out[2 * k * n:(2 * k + 1) * n] + out[(2 * k + 1) * n:(2 * k + 2) * n] for k in range(3)]

    most = route(surf_rows, hot_ref[...].astype(bf16), slot_ref[...])
    for k in range(3):
        surf_send[:, k, :] = most[k]
    surf_send[:, 3, :] = jnp.zeros((n, LANES), f32)

    lane = lax.broadcasted_iota(jnp.int32, (cy, LANES), 1)
    for side in range(4):
        take_face(2, side)
        weight = face_i[side] * OMEGA
        out = jnp.where(lane == 0, weight * recv23[1, side, 0], 0.0)
        for k in (1, 2):
            out = jnp.where(lane == k, pltpu.roll(weight * recv23[1, side, k], k, 1), out)
        xcol[side * cy:(side + 1) * cy, :] = out
    more = route(xcol[0:LANES, :].T[0:8], hot_face[...].astype(bf16), slot_face[...])
    for k in range(3):
        surf_send[:, k, :] = surf_send[:, k, :] + more[k]
    send_all(*surf)
    add_values(2, field)

    every(*meta).wait_recv()
    basis_u = pieces(meta_recv[:, 0, :])
    basis_v = pieces(meta_recv[:, 1, :])
    span_u = meta_recv[:, 2, :].astype(jnp.int32)
    span_v = meta_recv[:, 3, :].astype(jnp.int32)
    knot = lax.broadcasted_iota(jnp.int32, (NC, LANES), 0)

    def spline(span, basis, d):
        offset = knot - span[d:d + 1, :]
        out = jnp.where(offset == 0, basis[0][d:d + 1, :], 0.0)
        for index in range(1, 4):
            out = jnp.where(offset == index, basis[index][d:d + 1, :], out)
        return out

    for d in range(n):
        lanes = slice(d * LANES, (d + 1) * LANES)
        bu_ref[:, lanes] = spline(span_u, basis_u, d)
        high, low = split(spline(span_v, basis_v, d), 2)
        bv_ref[:NC, lanes] = high
        bv_ref[NC:, lanes] = low


    for side in range(4):
        @pl.when(sides[side][0])
        def _(side=side):
            face_copy(0, side, send1.at[side], recv1).wait_send()
            for turn in (1, 2):
                face_copy(turn, side, send_y.at[turn - 1, side], recv23.at[turn - 1]).wait_send()
    for index in range(4):
        @pl.when(corners[index][0])
        def _(index=index):
            corner_copy(index).wait_send()
    every(*meta).wait_send()
    every(*surf).wait_recv()
    every(*surf).wait_send()


def product(n, val, surf_ref, bu_ref, bv_ref, field, grad_ref, sem):
    store = pltpu.make_async_copy(val, field, sem)
    store.start()
    group = 8
    total = jnp.zeros((6 * NC, 2 * NC), jnp.float32)
    for first in range(0, n, group):
        lanes = slice(first * LANES, (first + group) * LANES)
        bu = bu_ref[:, lanes]
        left = jnp.concatenate(
            [
                bu * jnp.concatenate(
                    [surf_ref[d, k:k + 1, :] for d in range(first, first + group)],
                    axis=1,
                )
                for k in range(3)
            ],
            axis=0,
        )
        total = total + nt_dot(jnp.concatenate(split(left, 2), axis=0), bv_ref[:, lanes])
    for k in range(3):
        high, low = total[k * NC:(k + 1) * NC], total[(3 + k) * NC:(4 + k) * NC]
        grad_ref[k] = high[:, :NC] + high[:, NC:] + low[:, :NC] + low[:, NC:]
    store.wait()


def body(volume_sens, stiffness, patch_of_row, knot_spans, span_params):
    ngx, ngy = lax.axis_size("gx"), lax.axis_size("gy")
    n = ngx * ngy
    _, cx, cy, nz = volume_sens.shape
    rows = cx * cy
    step = cy + 2 * EDGE
    f32, bf16 = jnp.float32, jnp.bfloat16
    dma = pltpu.SemaphoreType.DMA
    vmem = pl.BlockSpec(memory_space=pltpu.VMEM)
    room = 62 * 2**20 - 4 * (3 * rows * nz + n * 4 * LANES + 2 * NC * n * LANES)
    found = pl.pallas_call(
        functools.partial(kernel, (ngx, ngy, cx, cy, rows)),
        out_shape=(
            pltpu.VMEM((3, rows, nz), f32),
            pltpu.VMEM((n, 4, LANES), f32),
            pltpu.VMEM((NC, n * LANES), f32),
            pltpu.VMEM((2 * NC, n * LANES), bf16),
        ),
        in_specs=[
            pl.BlockSpec(memory_space=pl.ANY),
            pl.BlockSpec(memory_space=pl.ANY),
            pl.BlockSpec(memory_space=pltpu.VMEM),
            pl.BlockSpec(memory_space=pltpu.VMEM),
            pl.BlockSpec(memory_space=pltpu.VMEM),
        ],
        out_specs=(vmem,) * 4,
        scratch_shapes=[
            pltpu.VMEM((3, rows, nz), f32),
            pltpu.VMEM((rows, nz), f32),
            pltpu.VMEM(((cx + 4) * step, nz), f32),
            pltpu.VMEM((rows, nz), f32),
            pltpu.VMEM((rows, nz), f32),
            pltpu.VMEM((3, rows, nz), f32),
            pltpu.VMEM((3, (cx + 2) * step, nz), f32),
            pltpu.VMEM((3, (cx + 2) * step, nz), f32),
            pltpu.VMEM((3, (cx + 2) * step, nz), f32),
            pltpu.VMEM((4, 5, cy, nz), f32),
            pltpu.VMEM((4, 5, cy, nz), f32),
            pltpu.VMEM((4, 8, nz), f32),
            pltpu.VMEM((4, 8, nz), f32),
            pltpu.VMEM((2, 4, 3, cy, nz), f32),
            pltpu.VMEM((2, 4, 3, cy, nz), f32),
            pltpu.VMEM((n, rows), f32),
            pltpu.VMEM((LANES, rows), bf16),
            pltpu.VMEM((rows, nz), f32),
            pltpu.VMEM((4, cy, nz), f32),
            pltpu.VMEM((4, cy, nz), f32),
            pltpu.VMEM((n, LANES), f32),
            pltpu.VMEM((LANES, LANES), bf16),
            pltpu.VMEM((n, 4, LANES), f32),
            pltpu.VMEM((n, 4, LANES), f32),
            pltpu.VMEM((n, 4, LANES), f32),
            dma((4,)),
            dma((12,)),
            dma((12,)),
            dma((4,)),
            dma((4,)),
            dma,
            dma,
            dma,
            dma,
        ],
        compiler_params=pltpu.CompilerParams(
            collective_id=0, has_side_effects=True, vmem_limit_bytes=room
        ),
    )(
        volume_sens.reshape(3, rows, nz),
        stiffness.reshape(rows, nz),
        patch_of_row.reshape(1, rows),
        knot_spans[0].T,
        span_params[0].T,
    )
    field, grads = pl.pallas_call(
        functools.partial(product, n),
        out_shape=(
            jax.ShapeDtypeStruct((3, rows, nz), f32),
            jax.ShapeDtypeStruct((3, NC, NC), f32),
        ),
        in_specs=[vmem] * 4,
        out_specs=(pl.BlockSpec(memory_space=pl.ANY), vmem),
        scratch_shapes=[dma],
        compiler_params=pltpu.CompilerParams(vmem_limit_bytes=32 * 2**20),
    )(*found)
    return field.reshape(volume_sens.shape), grads[None]


def solution(mesh):
    placed = (
        P(None, "gx", "gy", None),
        P("gx", "gy", None),
        P(("gx", "gy"), None, None),
        P(("gx", "gy"), None, None),
        P(("gx", "gy"), None, None),
    )
    return jax.shard_map(
        body,
        mesh=mesh,
        in_specs=placed,
        out_specs=(P(None, "gx", "gy", None), P(("gx", "gy"), None, None, None)),
        check_vma=False,
    )
```

```python
import functools

import jax
import jax.numpy as jnp
from jax import lax
from jax.experimental import pallas as pl
from jax.experimental.pallas import tpu as pltpu
from jax.sharding import PartitionSpec as P

SWEEPS = 3
NC = 64
OMEGA = 2.0 / 3.0
LANES = 128
EDGE = 8
UNROLL = 8
MESH = pl.DeviceIdType.MESH
NT = (((1,), (1,)), ((), ()))


def pieces(param):
    other = 1.0 - param
    square = param * param
    cube = square * param
    return [
        other * other * other / 6.0,
        (3.0 * cube - 6.0 * square + 4.0) / 6.0,
        (-3.0 * cube + 3.0 * square + 3.0 * param + 1.0) / 6.0,
        cube / 6.0,
    ]


def split(values, count):
    parts = []
    for _ in range(count):
        part = values.astype(jnp.bfloat16)
        parts.append(part)
        values = values - part.astype(jnp.float32)
    return parts


def nt_dot(left, right):
    return lax.dot_general(left, right, NT, preferred_element_type=jnp.float32)


def kernel(
    sizes,
    vol_hbm, stiff_hbm, patch_hbm, span_hbm, param_hbm,
    field, surf_recv, bu_ref, bv_ref,
    vol, cin, cpad, rd, wz, val, y0, y1, y2,
    send1, recv1, csend, crecv, send_y, recv23,
    hot_ref, slot_ref, xcol, face_w, face_i, hot_face, slot_face,
    patch_ref, span_ref, param_ref, meta_send, meta_recv, surf_send,
    in_sem, ssem, rsem, cssem, crsem, mssem, mrsem, ussem, ursem,
):
    ngx, ngy, cx, cy, rows = sizes
    n = ngx * ngy
    step = cy + 2 * EDGE
    gx, gy = lax.axis_index("gx"), lax.axis_index("gy")
    me = gx * ngy + gy
    f32, bf16 = jnp.float32, jnp.bfloat16

    load_c = pltpu.make_async_copy(stiff_hbm, cin, in_sem.at[0])
    load_v = [pltpu.make_async_copy(vol_hbm.at[k], vol.at[k], in_sem.at[1 + k]) for k in range(3)]
    load_rows = [
        pltpu.make_async_copy(src, dst, in_sem.at[4 + i])
        for i, (src, dst) in enumerate(
            ((patch_hbm, patch_ref), (span_hbm, span_ref), (param_hbm, param_ref))
        )
    ]
    load_rows[0].start()
    load_c.start()
    for k in range(3):
        load_v[k].start()
    load_rows[1].start()
    load_rows[2].start()

    barrier = pltpu.get_barrier_semaphore()

    def greet(i, carry):
        to = lax.rem(me + i, n)
        pl.semaphore_signal(barrier, inc=1, device_id=(to // ngy, lax.rem(to, ngy)), device_id_type=MESH)
        return carry

    lax.fori_loop(1, n, greet, 0)

    sides = (
        (gx > 0, (jnp.maximum(gx - 1, 0), gy), 1),
        (gx < ngx - 1, (jnp.minimum(gx + 1, ngx - 1), gy), 0),
        (gy > 0, (gx, jnp.maximum(gy - 1, 0)), 3),
        (gy < ngy - 1, (gx, jnp.minimum(gy + 1, ngy - 1)), 2),
    )

    def face_copy(turn, side, src, dst):
        return pltpu.make_async_remote_copy(
            src_ref=src,
            dst_ref=dst.at[sides[side][2]],
            send_sem=ssem.at[turn * 4 + side],
            recv_sem=rsem.at[turn * 4 + sides[side][2]],
            device_id=sides[side][1],
            device_id_type=MESH,
        )

    def face_wait(turn, side, src, dst):
        return pltpu.make_async_remote_copy(
            src_ref=src,
            dst_ref=dst.at[side],
            send_sem=ssem.at[turn * 4 + side],
            recv_sem=rsem.at[turn * 4 + side],
            device_id=sides[side][1],
            device_id_type=MESH,
        )

    corners = []
    for a in (0, 1):
        for b in (0, 1):
            okay = jnp.logical_and(sides[a][0], sides[2 + b][0])
            corners.append((okay, (sides[a][1][0], sides[2 + b][1][1])))

    def corner_copy(index):
        return pltpu.make_async_remote_copy(
            src_ref=csend.at[index],
            dst_ref=crecv.at[3 - index],
            send_sem=cssem.at[index],
            recv_sem=crsem.at[3 - index],
            device_id=corners[index][1],
            device_id_type=MESH,
        )

    def corner_wait(index):
        return pltpu.make_async_remote_copy(
            src_ref=csend.at[index],
            dst_ref=crecv.at[index],
            send_sem=cssem.at[index],
            recv_sem=crsem.at[index],
            device_id=corners[index][1],
            device_id_type=MESH,
        )

    for side in range(4):
        @pl.when(jnp.logical_not(sides[side][0]))
        def _(side=side):
            recv1[side] = jnp.zeros(recv1.shape[1:], f32)
            for turn in range(2):
                recv23[turn, side] = jnp.zeros(recv23.shape[2:], f32)
    for index in range(4):
        @pl.when(jnp.logical_not(corners[index][0]))
        def _(index=index):
            crecv[index] = jnp.zeros(crecv.shape[1:], f32)

    def clear(ix, carry):
        base = pl.multiple_of(ix * step, 8)
        for y in (y0, y1, y2):
            y[:, pl.ds(base, EDGE), :] = jnp.zeros((3, EDGE, LANES), f32)
            y[:, pl.ds(base + EDGE + cy, EDGE), :] = jnp.zeros((3, EDGE, LANES), f32)
        cpad[pl.ds(base + step, EDGE), :] = jnp.zeros((EDGE, LANES), f32)
        cpad[pl.ds(base + step + EDGE + cy, EDGE), :] = jnp.zeros((EDGE, LANES), f32)
        return carry

    lax.fori_loop(0, cx + 2, clear, 0)
    for y in (y0, y1, y2):
        y[:, pl.ds(EDGE, cy), :] = jnp.zeros((3, cy, LANES), f32)
        y[:, pl.ds((cx + 1) * step + EDGE, cy), :] = jnp.zeros((3, cy, LANES), f32)
    for layer in (0, 1, cx + 2, cx + 3):
        cpad[pl.ds(layer * step + EDGE, cy), :] = jnp.zeros((cy, LANES), f32)

    load_rows[0].wait()
    patch = patch_ref[...]
    hot = (lax.broadcasted_iota(jnp.int32, (n, rows), 0) == patch).astype(f32)
    hot_ref[...] = hot
    upper = (
        lax.broadcasted_iota(jnp.int32, (LANES, LANES), 0)
        <= lax.broadcasted_iota(jnp.int32, (LANES, LANES), 1)
    ).astype(f32).astype(bf16)
    before = jnp.zeros((n, 1), f32)
    for chunk in range(rows // LANES):
        part = hot[:, chunk * LANES:(chunk + 1) * LANES]
        count = jnp.dot(part.astype(bf16), upper, preferred_element_type=f32)
        rank = jnp.sum(part * (count + before), axis=0, keepdims=True) - 1.0
        before = before + count[:, LANES - 1:LANES]
        place = lax.broadcasted_iota(jnp.int32, (LANES, LANES), 0)
        slot_ref[:, chunk * LANES:(chunk + 1) * LANES] = (
            (place == rank.astype(jnp.int32)).astype(f32).astype(bf16)
        )

    load_c.wait()
    last = (cx - 1) * cy
    for deep in range(2):
        send1[0, 3 + deep] = cin[deep * cy:(deep + 1) * cy]
        send1[1, 3 + deep] = cin[last - deep * cy:last - deep * cy + cy]
        send1[2, 3 + deep] = cin[pl.ds(deep, cx, stride=cy)]
        send1[3, 3 + deep] = cin[pl.ds(cy - 1 - deep, cx, stride=cy)]
    for index in range(4):
        row = (index // 2) * last + (index % 2) * (cy - 1)
        csend[index] = jnp.broadcast_to(cin[row:row + 1], (8, LANES))

    for k in range(3):
        load_v[k].wait()
        send1[0, k] = vol[k, 0:cy]
        send1[1, k] = vol[k, last:last + cy]
        send1[2, k] = vol[k, pl.ds(0, cx, stride=cy)]
        send1[3, k] = vol[k, pl.ds(cy - 1, cx, stride=cy)]

    pl.semaphore_wait(barrier, n - 1)
    for side in (2, 3, 0, 1):
        @pl.when(sides[side][0])
        def _(side=side):
            face_copy(0, side, send1.at[side], recv1).start()
    for index in range(4):
        @pl.when(corners[index][0])
        def _(index=index):
            corner_copy(index).start()

    def all_copy(src, dst, sems, other, landing):
        return pltpu.make_async_remote_copy(
            src_ref=src.at[other],
            dst_ref=dst.at[landing],
            send_sem=sems[0],
            recv_sem=sems[1],
            device_id=(other // ngy, lax.rem(other, ngy)),
            device_id_type=MESH,
        )

    def send_all(src, dst, sems):
        def go(i, carry):
            all_copy(src, dst, sems, lax.rem(me + i, n), me).start()
            return carry

        lax.fori_loop(1, n, go, 0)
        dst[me] = src[me]

    def every(src, dst, sems):
        other = lax.rem(me + 1, n)
        return pltpu.make_async_remote_copy(
            src_ref=src.at[pl.ds(0, n - 1)],
            dst_ref=dst.at[pl.ds(0, n - 1)],
            send_sem=sems[0],
            recv_sem=sems[1],
            device_id=(other // ngy, lax.rem(other, ngy)),
            device_id_type=MESH,
        )

    meta = (meta_send, meta_recv, (mssem, mrsem))
    surf = (surf_send, surf_recv, (ussem, ursem))

    def fill(ix, carry):
        to = pl.multiple_of((ix + 2) * step + EDGE, 8)
        cpad[pl.ds(to, cy), :] = cin[pl.ds(pl.multiple_of(ix * cy, 8), cy), :] * (OMEGA / 2)
        return carry

    lax.fori_loop(0, cx, fill, 0, unroll=UNROLL)
    def inverse(center, others):
        lane = lax.broadcasted_iota(jnp.int32, center.shape, 1)
        above = jnp.where(lane == LANES - 1, 0.0, pltpu.roll(center, LANES - 1, 1))
        below = jnp.where(lane == 0, 0.0, pltpu.roll(center, 1, 1))
        total = 6.0 * center + above + below
        for other in others:
            total = total + other
        return OMEGA / total, above

    def scale(it, carry):
        done = []
        for u in range(UNROLL):
            ix = it * UNROLL + u
            at = pl.multiple_of((ix + 2) * step + EDGE, 8)
            to = pl.multiple_of(ix * cy, 8)
            center = cpad[pl.ds(at, cy), :]
            inv, above = inverse(
                center,
                [cpad[pl.ds(at + d, cy), :] for d in (-step, step, -1, 1)],
            )
            lane = lax.broadcasted_iota(jnp.int32, center.shape, 1)
            up = jnp.where(lane == LANES - 1, 0.0, center + above)
            done.append((at, to, inv, up, vol[:, pl.ds(to, cy), :] * inv[None]))
        for at, to, inv, up, scaled in done:
            rd[pl.ds(to, cy), :] = inv
            wz[pl.ds(to, cy), :] = up
            y0[:, pl.ds(pl.multiple_of(at - step, 8), cy), :] = scaled
        return carry

    lax.fori_loop(0, cx // UNROLL, scale, 0)

    def sweep(vsrc, vdst, ysrc, ydst):
        def layers(it, carry):
            done = []
            for u in range(UNROLL):
                ix = it * UNROLL + u
                at = pl.multiple_of((ix + 1) * step + EDGE, 8)
                ct = pl.multiple_of((ix + 2) * step + EDGE, 8)
                to = pl.multiple_of(ix * cy, 8)
                center = cpad[pl.ds(ct, cy), :]
                up = wz[pl.ds(to, cy), :][None]
                mid = ysrc[:, pl.ds(at, cy), :]
                total = up * pltpu.roll(mid, LANES - 1, 2) + pltpu.roll(up * mid, 1, 2)
                for d in (step, -step, 1, -1):
                    weight = center + cpad[pl.ds(ct + d, cy), :]
                    total = total + weight[None] * ysrc[:, pl.ds(at + d, cy), :]
                new = vol[:, pl.ds(to, cy), :] + (1.0 - OMEGA) * vsrc[:, pl.ds(to, cy), :] + total
                done.append((at, to, new))
            for at, to, new in done:
                vdst[:, pl.ds(to, cy), :] = new
                if ydst is not None:
                    ydst[:, pl.ds(at, cy), :] = new * rd[pl.ds(to, cy), :][None]
            return carry

        lax.fori_loop(0, cx // UNROLL, layers, 0)

    def line(kind, j, height):
        if kind == 0:
            base = (j + height) * step + EDGE
            return lambda d: pl.ds(base + d, cy)
        base = height * step + EDGE + j
        return lambda d: pl.ds(base + d, cx, stride=step)

    def flat_line(kind, j):
        return pl.ds(j * cy, cy) if kind == 0 else pl.ds(j, cx, stride=cy)

    def scale_line(kind, j):
        c, flat, yl = line(kind, j, 2), flat_line(kind, j), line(kind, j, 1)
        inv, _ = inverse(cpad[c(0), :], [cpad[c(d), :] for d in (-step, step, -1, 1)])
        rd[flat, :] = inv
        for k in range(3):
            y0[k, yl(0), :] = vol[k, flat, :] * inv

    def sweep_line(kind, j, side=None):
        c, flat, yl = line(kind, j, 2), flat_line(kind, j), line(kind, j, 1)
        center, up, inv = cpad[c(0), :], wz[flat, :], rd[flat, :]
        weights = [(d, center + cpad[c(d), :]) for d in (step, -step, 1, -1)]
        done = []
        for k in range(3):
            mid, first = y0[k, yl(0), :], vol[k, flat, :]
            total = up * pltpu.roll(mid, LANES - 1, 1) + pltpu.roll(up * mid, 1, 1)
            for d, weight in weights:
                total = total + weight * y0[k, yl(d), :]
            done.append(first + (1.0 - OMEGA) * first + total)
        for k in range(3):
            field[k, flat, :] = done[k]
            y1[k, yl(0), :] = done[k] * inv
            if side is not None:
                send_y[0, side, k] = done[k] * inv
        if side is not None:
            send_face(1, side)

    def send_face(turn, side):
        @pl.when(sides[side][0])
        def _():
            face_copy(turn, side, send_y.at[turn - 1, side], recv23.at[turn - 1]).start()

    def take_face(turn, side):
        @pl.when(sides[side][0])
        def _():
            face_wait(turn, side, send_y.at[turn - 1, side], recv23.at[turn - 1]).wait_recv()

    ends = ((0, 0), (0, cx - 1), (1, 0), (1, cy - 1))
    beside = ((0, 1), (0, cx - 2), (1, 1), (1, cy - 2))

    def add_values(turn, dst):
        for side in range(4):
            flat = flat_line(*ends[side])
            for k in range(3):
                dst[k, flat, :] = dst[k, flat, :] + face_w[side] * recv23[turn - 1, side, k]

    sweep(vol, field, y0, y1)
    for side in range(4):
        @pl.when(sides[side][0])
        def _(side=side):
            face_wait(0, side, send1.at[side], recv1).wait_recv()
    for index in range(4):
        @pl.when(corners[index][0])
        def _(index=index):
            corner_wait(index).wait_recv()
    half = OMEGA / 2
    for deep in range(2):
        low, high = (1 - deep) * step + EDGE, (cx + 2 + deep) * step + EDGE
        cpad[low:low + cy, :] = recv1[0, 3 + deep] * half
        cpad[high:high + cy, :] = recv1[1, 3 + deep] * half
        cpad[pl.ds(2 * step + EDGE - 1 - deep, cx, stride=step), :] = recv1[2, 3 + deep] * half
        cpad[pl.ds(2 * step + EDGE + cy + deep, cx, stride=step), :] = recv1[3, 3 + deep] * half
    for index in range(4):
        row = (1 + (index // 2) * (cx + 1)) * step + EDGE - 1 + (index % 2) * (cy + 1)
        cpad[row:row + 1, :] = crecv[index, 0:1] * half

    for kind, j in ends:
        scale_line(kind, j)
    for side in range(4):
        if side < 2:
            at = (1 + side * (cx + 1)) * step + EDGE
            inv, _ = inverse(
                cpad[at:at + cy, :],
                [cpad[at + d:at + d + cy, :] for d in (-step, step, -1, 1)],
            )
            for k in range(3):
                y0[k, at - step:at - step + cy, :] = recv1[side, k] * inv
        else:
            at = 2 * step + EDGE - 1 + (side - 2) * (cy + 1)
            inv, _ = inverse(
                cpad[pl.ds(at, cx, stride=step), :],
                [cpad[pl.ds(at + d, cx, stride=step), :] for d in (-step, step, -1, 1)],
            )
            for k in range(3):
                y0[k, pl.ds(at - step, cx, stride=step), :] = recv1[side, k] * inv

    for side in (2, 3, 0, 1):
        sweep_line(*ends[side], side)
    for kind, j in beside:
        sweep_line(kind, j)
    for side, out in enumerate((-step, step, -1, 1)):
        at = line(*ends[side], 2)
        weight = cpad[at(0), :] + cpad[at(out), :]
        face_w[side] = weight
        face_i[side] = weight * rd[flat_line(*ends[side]), :]
    sweep(field, val, y1, y2)
    face = lax.broadcasted_iota(jnp.int32, (1, LANES), 1)
    part = lax.rem(face, cy)
    where = jnp.where(face < cy, part, last + part)
    where = jnp.where(face >= 2 * cy, part * cy, where)
    where = jnp.where(face >= 3 * cy, part * cy + cy - 1, where)
    pick = (lax.broadcasted_iota(jnp.int32, (rows, LANES), 0) == where).astype(f32).astype(bf16)
    hot_face[...] = jnp.dot(hot_ref[...].astype(bf16), pick, preferred_element_type=f32)
    slot_face[...] = jnp.dot(slot_ref[...], pick, preferred_element_type=f32).astype(bf16)

    load_rows[1].wait()
    load_rows[2].wait()
    hot16 = hot_ref[...].astype(bf16)
    slots = slot_ref[...]
    stack = []
    for q in range(2):
        stack += split(param_ref[q:q + 1, :], 2)
    for q in range(2):
        stack.append(span_ref[q:q + 1, :].astype(f32).astype(bf16))
    out = nt_dot(jnp.concatenate([hot16 * part for part in stack], axis=0), slots)
    out = [out[i * n:(i + 1) * n] for i in range(6)]
    meta_send[:, 0, :] = out[0] + out[1]
    meta_send[:, 1, :] = out[2] + out[3]
    meta_send[:, 2, :] = out[4]
    meta_send[:, 3, :] = out[5]
    send_all(*meta)

    for side in (0, 1, 2, 3):
        take_face(1, side)
        at = line(*ends[side], 1)(0)
        for k in range(3):
            new = y2[k, at, :] + face_i[side] * recv23[0, side, k]
            y2[k, at, :] = new
            if side > 1:
                send_y[1, side, k] = new
        if side > 1:
            send_face(2, side)
    for side in (0, 1):
        at = line(*ends[side], 1)(0)
        for k in range(3):
            send_y[1, side, k] = y2[k, at, :]
        send_face(2, side)
    add_values(1, val)
    sweep(val, field, y2, None)


    def surface(ix, carry):
        to = pl.ds(pl.multiple_of(ix * cy, 8), cy)
        lane = lax.broadcasted_iota(jnp.int32, (cy, LANES), 1)
        inv = rd[to, :] * OMEGA
        out = jnp.where(lane == 0, field[0, to, :] * inv, 0.0)
        for k in (1, 2):
            out = jnp.where(lane == k, pltpu.roll(field[k, to, :] * inv, k, 1), out)
        xcol[to, :] = out
        return carry

    lax.fori_loop(0, cx, surface, 0, unroll=UNROLL)
    surf_rows = jnp.concatenate(
        [xcol[c * LANES:(c + 1) * LANES, :].T[0:8] for c in range(rows // LANES)], axis=1
    )
    def route(values, hot16, slots):
        stack = []
        for k in range(3):
            stack += split(values[k:k + 1, :], 2)
        out = nt_dot(jnp.concatenate([hot16 * part for part in stack], axis=0), slots)
        return [out[2 * k * n:(2 * k + 1) * n] + out[(2 * k + 1) * n:(2 * k + 2) * n] for k in range(3)]

    most = route(surf_rows, hot_ref[...].astype(bf16), slot_ref[...])
    for k in range(3):
        surf_send[:, k, :] = most[k]
    surf_send[:, 3, :] = jnp.zeros((n, LANES), f32)

    lane = lax.broadcasted_iota(jnp.int32, (cy, LANES), 1)
    for side in range(4):
        take_face(2, side)
        weight = face_i[side] * OMEGA
        out = jnp.where(lane == 0, weight * recv23[1, side, 0], 0.0)
        for k in (1, 2):
            out = jnp.where(lane == k, pltpu.roll(weight * recv23[1, side, k], k, 1), out)
        xcol[side * cy:(side + 1) * cy, :] = out
    more = route(xcol[0:LANES, :].T[0:8], hot_face[...].astype(bf16), slot_face[...])
    for k in range(3):
        surf_send[:, k, :] = surf_send[:, k, :] + more[k]
    send_all(*surf)
    add_values(2, field)

    every(*meta).wait_recv()
    basis_u = pieces(meta_recv[:, 0, :])
    basis_v = pieces(meta_recv[:, 1, :])
    span_u = meta_recv[:, 2, :].astype(jnp.int32)
    span_v = meta_recv[:, 3, :].astype(jnp.int32)
    knot = lax.broadcasted_iota(jnp.int32, (NC, LANES), 0)

    def spline(span, basis, d):
        offset = knot - span[d:d + 1, :]
        out = jnp.where(offset == 0, basis[0][d:d + 1, :], 0.0)
        for index in range(1, 4):
            out = jnp.where(offset == index, basis[index][d:d + 1, :], out)
        return out

    for d in range(n):
        lanes = slice(d * LANES, (d + 1) * LANES)
        bu_ref[:, lanes] = spline(span_u, basis_u, d)
        high, low = split(spline(span_v, basis_v, d), 2)
        bv_ref[:NC, lanes] = high
        bv_ref[NC:, lanes] = low


    for side in range(4):
        @pl.when(sides[side][0])
        def _(side=side):
            face_copy(0, side, send1.at[side], recv1).wait_send()
            for turn in (1, 2):
                face_copy(turn, side, send_y.at[turn - 1, side], recv23.at[turn - 1]).wait_send()
    for index in range(4):
        @pl.when(corners[index][0])
        def _(index=index):
            corner_copy(index).wait_send()
    every(*meta).wait_send()
    every(*surf).wait_recv()
    every(*surf).wait_send()


def product(n, val, surf_ref, bu_ref, bv_ref, field, grad_ref, sem):
    store = pltpu.make_async_copy(val, field, sem)
    store.start()
    group = 8
    total = jnp.zeros((6 * NC, 2 * NC), jnp.float32)
    for first in range(0, n, group):
        lanes = slice(first * LANES, (first + group) * LANES)
        bu = bu_ref[:, lanes]
        left = jnp.concatenate(
            [
                bu * jnp.concatenate(
                    [surf_ref[d, k:k + 1, :] for d in range(first, first + group)],
                    axis=1,
                )
                for k in range(3)
            ],
            axis=0,
        )
        total = total + nt_dot(jnp.concatenate(split(left, 2), axis=0), bv_ref[:, lanes])
    for k in range(3):
        high, low = total[k * NC:(k + 1) * NC], total[(3 + k) * NC:(4 + k) * NC]
        grad_ref[k] = high[:, :NC] + high[:, NC:] + low[:, :NC] + low[:, NC:]
    store.wait()


def body(volume_sens, stiffness, patch_of_row, knot_spans, span_params):
    ngx, ngy = lax.axis_size("gx"), lax.axis_size("gy")
    n = ngx * ngy
    _, cx, cy, nz = volume_sens.shape
    rows = cx * cy
    step = cy + 2 * EDGE
    f32, bf16 = jnp.float32, jnp.bfloat16
    dma = pltpu.SemaphoreType.DMA
    vmem = pl.BlockSpec(memory_space=pltpu.VMEM)
    room = 62 * 2**20 - 4 * (3 * rows * nz + n * 4 * LANES + 2 * NC * n * LANES)
    found = pl.pallas_call(
        functools.partial(kernel, (ngx, ngy, cx, cy, rows)),
        out_shape=(
            pltpu.VMEM((3, rows, nz), f32),
            pltpu.VMEM((n, 4, LANES), f32),
            pltpu.VMEM((NC, n * LANES), f32),
            pltpu.VMEM((2 * NC, n * LANES), bf16),
        ),
        in_specs=[
            pl.BlockSpec(memory_space=pl.ANY),
            pl.BlockSpec(memory_space=pl.ANY),
            pl.BlockSpec(memory_space=pl.ANY),
            pl.BlockSpec(memory_space=pl.ANY),
            pl.BlockSpec(memory_space=pl.ANY),
        ],
        out_specs=(vmem,) * 4,
        scratch_shapes=[
            pltpu.VMEM((3, rows, nz), f32),
            pltpu.VMEM((rows, nz), f32),
            pltpu.VMEM(((cx + 4) * step, nz), f32),
            pltpu.VMEM((rows, nz), f32),
            pltpu.VMEM((rows, nz), f32),
            pltpu.VMEM((3, rows, nz), f32),
            pltpu.VMEM((3, (cx + 2) * step, nz), f32),
            pltpu.VMEM((3, (cx + 2) * step, nz), f32),
            pltpu.VMEM((3, (cx + 2) * step, nz), f32),
            pltpu.VMEM((4, 5, cy, nz), f32),
            pltpu.VMEM((4, 5, cy, nz), f32),
            pltpu.VMEM((4, 8, nz), f32),
            pltpu.VMEM((4, 8, nz), f32),
            pltpu.VMEM((2, 4, 3, cy, nz), f32),
            pltpu.VMEM((2, 4, 3, cy, nz), f32),
            pltpu.VMEM((n, rows), f32),
            pltpu.VMEM((LANES, rows), bf16),
            pltpu.VMEM((rows, nz), f32),
            pltpu.VMEM((4, cy, nz), f32),
            pltpu.VMEM((4, cy, nz), f32),
            pltpu.VMEM((n, LANES), f32),
            pltpu.VMEM((LANES, LANES), bf16),
            pltpu.VMEM((1, rows), jnp.int32),
            pltpu.VMEM((2, rows), jnp.int32),
            pltpu.VMEM((2, rows), f32),
            pltpu.VMEM((n, 4, LANES), f32),
            pltpu.VMEM((n, 4, LANES), f32),
            pltpu.VMEM((n, 4, LANES), f32),
            dma((7,)),
            dma((12,)),
            dma((12,)),
            dma((4,)),
            dma((4,)),
            dma,
            dma,
            dma,
            dma,
        ],
        compiler_params=pltpu.CompilerParams(
            collective_id=0, has_side_effects=True, vmem_limit_bytes=room
        ),
    )(
        volume_sens.reshape(3, rows, nz),
        stiffness.reshape(rows, nz),
        patch_of_row.reshape(1, rows),
        knot_spans[0].T,
        span_params[0].T,
    )
    field, grads = pl.pallas_call(
        functools.partial(product, n),
        out_shape=(
            jax.ShapeDtypeStruct((3, rows, nz), f32),
            jax.ShapeDtypeStruct((3, NC, NC), f32),
        ),
        in_specs=[vmem] * 4,
        out_specs=(pl.BlockSpec(memory_space=pl.ANY), vmem),
        scratch_shapes=[dma],
        compiler_params=pltpu.CompilerParams(vmem_limit_bytes=32 * 2**20),
    )(*found)
    return field.reshape(volume_sens.shape), grads[None]


def solution(mesh):
    placed = (
        P(None, "gx", "gy", None),
        P("gx", "gy", None),
        P(("gx", "gy"), None, None),
        P(("gx", "gy"), None, None),
        P(("gx", "gy"), None, None),
    )
    return jax.shard_map(
        body,
        mesh=mesh,
        in_specs=placed,
        out_specs=(P(None, "gx", "gy", None), P(("gx", "gy"), None, None, None)),
        check_vma=False,
    )
```

```python
import functools

import jax
import jax.numpy as jnp
from jax import lax
from jax.experimental import pallas as pl
from jax.experimental.pallas import tpu as pltpu
from jax.sharding import PartitionSpec as P

SWEEPS = 3
NC = 64
OMEGA = 2.0 / 3.0
LANES = 128
EDGE = 8
UNROLL = 8
MESH = pl.DeviceIdType.MESH
NT = (((1,), (1,)), ((), ()))


def pieces(param):
    other = 1.0 - param
    square = param * param
    cube = square * param
    return [
        other * other * other / 6.0,
        (3.0 * cube - 6.0 * square + 4.0) / 6.0,
        (-3.0 * cube + 3.0 * square + 3.0 * param + 1.0) / 6.0,
        cube / 6.0,
    ]


def split(values, count):
    parts = []
    for _ in range(count):
        part = values.astype(jnp.bfloat16)
        parts.append(part)
        values = values - part.astype(jnp.float32)
    return parts


def nt_dot(left, right):
    return lax.dot_general(left, right, NT, preferred_element_type=jnp.float32)


def kernel(
    sizes,
    vol_hbm, stiff_hbm, patch_hbm, span_hbm, param_hbm,
    field, surf_recv, bu_ref, bv_ref,
    vol, cin, cpad, rd, wz, val, y0, y1, y2,
    send1, recv1, csend, crecv, send_y, recv23,
    hot_ref, slot_ref, xcol, face_w, face_i, hot_face, slot_face,
    patch_ref, span_ref, param_ref, meta_send, meta_recv, surf_send,
    in_sem, ssem, rsem, cssem, crsem, mssem, mrsem, ussem, ursem,
):
    ngx, ngy, cx, cy, rows = sizes
    n = ngx * ngy
    step = cy + 2 * EDGE
    gx, gy = lax.axis_index("gx"), lax.axis_index("gy")
    me = gx * ngy + gy
    f32, bf16 = jnp.float32, jnp.bfloat16

    load_c = pltpu.make_async_copy(stiff_hbm, cin, in_sem.at[0])
    load_v = [pltpu.make_async_copy(vol_hbm.at[k], vol.at[k], in_sem.at[1 + k]) for k in range(3)]
    load_rows = [
        pltpu.make_async_copy(src, dst, in_sem.at[4 + i])
        for i, (src, dst) in enumerate(
            ((patch_hbm, patch_ref), (span_hbm, span_ref), (param_hbm, param_ref))
        )
    ]
    load_rows[0].start()
    load_c.start()
    for k in range(3):
        load_v[k].start()
    load_rows[1].start()
    load_rows[2].start()

    barrier = pltpu.get_barrier_semaphore()

    def greet(i, carry):
        to = lax.rem(me + i, n)
        pl.semaphore_signal(barrier, inc=1, device_id=(to // ngy, lax.rem(to, ngy)), device_id_type=MESH)
        return carry

    lax.fori_loop(1, n, greet, 0, unroll=True)

    sides = (
        (gx > 0, (jnp.maximum(gx - 1, 0), gy), 1),
        (gx < ngx - 1, (jnp.minimum(gx + 1, ngx - 1), gy), 0),
        (gy > 0, (gx, jnp.maximum(gy - 1, 0)), 3),
        (gy < ngy - 1, (gx, jnp.minimum(gy + 1, ngy - 1)), 2),
    )

    def face_copy(turn, side, src, dst):
        return pltpu.make_async_remote_copy(
            src_ref=src,
            dst_ref=dst.at[sides[side][2]],
            send_sem=ssem.at[turn * 4 + side],
            recv_sem=rsem.at[turn * 4 + sides[side][2]],
            device_id=sides[side][1],
            device_id_type=MESH,
        )

    def face_wait(turn, side, src, dst):
        return pltpu.make_async_remote_copy(
            src_ref=src,
            dst_ref=dst.at[side],
            send_sem=ssem.at[turn * 4 + side],
            recv_sem=rsem.at[turn * 4 + side],
            device_id=sides[side][1],
            device_id_type=MESH,
        )

    corners = []
    for a in (0, 1):
        for b in (0, 1):
            okay = jnp.logical_and(sides[a][0], sides[2 + b][0])
            corners.append((okay, (sides[a][1][0], sides[2 + b][1][1])))

    def corner_copy(index):
        return pltpu.make_async_remote_copy(
            src_ref=csend.at[index],
            dst_ref=crecv.at[3 - index],
            send_sem=cssem.at[index],
            recv_sem=crsem.at[3 - index],
            device_id=corners[index][1],
            device_id_type=MESH,
        )

    def corner_wait(index):
        return pltpu.make_async_remote_copy(
            src_ref=csend.at[index],
            dst_ref=crecv.at[index],
            send_sem=cssem.at[index],
            recv_sem=crsem.at[index],
            device_id=corners[index][1],
            device_id_type=MESH,
        )

    for side in range(4):
        @pl.when(jnp.logical_not(sides[side][0]))
        def _(side=side):
            recv1[side] = jnp.zeros(recv1.shape[1:], f32)
            for turn in range(2):
                recv23[turn, side] = jnp.zeros(recv23.shape[2:], f32)
    for index in range(4):
        @pl.when(jnp.logical_not(corners[index][0]))
        def _(index=index):
            crecv[index] = jnp.zeros(crecv.shape[1:], f32)

    def clear(ix, carry):
        base = pl.multiple_of(ix * step, 8)
        for y in (y0, y1, y2):
            y[:, pl.ds(base, EDGE), :] = jnp.zeros((3, EDGE, LANES), f32)
            y[:, pl.ds(base + EDGE + cy, EDGE), :] = jnp.zeros((3, EDGE, LANES), f32)
        cpad[pl.ds(base + step, EDGE), :] = jnp.zeros((EDGE, LANES), f32)
        cpad[pl.ds(base + step + EDGE + cy, EDGE), :] = jnp.zeros((EDGE, LANES), f32)
        return carry

    lax.fori_loop(0, cx + 2, clear, 0)
    for y in (y0, y1, y2):
        y[:, pl.ds(EDGE, cy), :] = jnp.zeros((3, cy, LANES), f32)
        y[:, pl.ds((cx + 1) * step + EDGE, cy), :] = jnp.zeros((3, cy, LANES), f32)
    for layer in (0, 1, cx + 2, cx + 3):
        cpad[pl.ds(layer * step + EDGE, cy), :] = jnp.zeros((cy, LANES), f32)

    load_rows[0].wait()
    patch = patch_ref[...]
    hot = (lax.broadcasted_iota(jnp.int32, (n, rows), 0) == patch).astype(f32)
    hot_ref[...] = hot
    upper = (
        lax.broadcasted_iota(jnp.int32, (LANES, LANES), 0)
        <= lax.broadcasted_iota(jnp.int32, (LANES, LANES), 1)
    ).astype(f32).astype(bf16)
    before = jnp.zeros((n, 1), f32)
    for chunk in range(rows // LANES):
        part = hot[:, chunk * LANES:(chunk + 1) * LANES]
        count = jnp.dot(part.astype(bf16), upper, preferred_element_type=f32)
        rank = jnp.sum(part * (count + before), axis=0, keepdims=True) - 1.0
        before = before + count[:, LANES - 1:LANES]
        place = lax.broadcasted_iota(jnp.int32, (LANES, LANES), 0)
        slot_ref[:, chunk * LANES:(chunk + 1) * LANES] = (
            (place == rank.astype(jnp.int32)).astype(f32).astype(bf16)
        )

    load_c.wait()
    last = (cx - 1) * cy
    for deep in range(2):
        send1[0, 3 + deep] = cin[deep * cy:(deep + 1) * cy]
        send1[1, 3 + deep] = cin[last - deep * cy:last - deep * cy + cy]
        send1[2, 3 + deep] = cin[pl.ds(deep, cx, stride=cy)]
        send1[3, 3 + deep] = cin[pl.ds(cy - 1 - deep, cx, stride=cy)]
    for index in range(4):
        row = (index // 2) * last + (index % 2) * (cy - 1)
        csend[index] = jnp.broadcast_to(cin[row:row + 1], (8, LANES))

    for k in range(3):
        load_v[k].wait()
        send1[0, k] = vol[k, 0:cy]
        send1[1, k] = vol[k, last:last + cy]
        send1[2, k] = vol[k, pl.ds(0, cx, stride=cy)]
        send1[3, k] = vol[k, pl.ds(cy - 1, cx, stride=cy)]

    pl.semaphore_wait(barrier, n - 1)
    for side in (2, 3, 0, 1):
        @pl.when(sides[side][0])
        def _(side=side):
            face_copy(0, side, send1.at[side], recv1).start()
    for index in range(4):
        @pl.when(corners[index][0])
        def _(index=index):
            corner_copy(index).start()

    def all_copy(src, dst, sems, other, landing):
        return pltpu.make_async_remote_copy(
            src_ref=src.at[other],
            dst_ref=dst.at[landing],
            send_sem=sems[0],
            recv_sem=sems[1],
            device_id=(other // ngy, lax.rem(other, ngy)),
            device_id_type=MESH,
        )

    def send_all(src, dst, sems):
        def go(i, carry):
            all_copy(src, dst, sems, lax.rem(me + i, n), me).start()
            return carry

        lax.fori_loop(1, n, go, 0, unroll=True)
        dst[me] = src[me]

    def every(src, dst, sems):
        other = lax.rem(me + 1, n)
        return pltpu.make_async_remote_copy(
            src_ref=src.at[pl.ds(0, n - 1)],
            dst_ref=dst.at[pl.ds(0, n - 1)],
            send_sem=sems[0],
            recv_sem=sems[1],
            device_id=(other // ngy, lax.rem(other, ngy)),
            device_id_type=MESH,
        )

    meta = (meta_send, meta_recv, (mssem, mrsem))
    surf = (surf_send, surf_recv, (ussem, ursem))

    def fill(ix, carry):
        to = pl.multiple_of((ix + 2) * step + EDGE, 8)
        cpad[pl.ds(to, cy), :] = cin[pl.ds(pl.multiple_of(ix * cy, 8), cy), :] * (OMEGA / 2)
        return carry

    lax.fori_loop(0, cx, fill, 0, unroll=UNROLL)
    def inverse(center, others):
        lane = lax.broadcasted_iota(jnp.int32, center.shape, 1)
        above = jnp.where(lane == LANES - 1, 0.0, pltpu.roll(center, LANES - 1, 1))
        below = jnp.where(lane == 0, 0.0, pltpu.roll(center, 1, 1))
        total = 6.0 * center + above + below
        for other in others:
            total = total + other
        return OMEGA / total, above

    def scale(it, carry):
        done = []
        for u in range(UNROLL):
            ix = it * UNROLL + u
            at = pl.multiple_of((ix + 2) * step + EDGE, 8)
            to = pl.multiple_of(ix * cy, 8)
            center = cpad[pl.ds(at, cy), :]
            inv, above = inverse(
                center,
                [cpad[pl.ds(at + d, cy), :] for d in (-step, step, -1, 1)],
            )
            lane = lax.broadcasted_iota(jnp.int32, center.shape, 1)
            up = jnp.where(lane == LANES - 1, 0.0, center + above)
            done.append((at, to, inv, up, vol[:, pl.ds(to, cy), :] * inv[None]))
        for at, to, inv, up, scaled in done:
            rd[pl.ds(to, cy), :] = inv
            wz[pl.ds(to, cy), :] = up
            y0[:, pl.ds(pl.multiple_of(at - step, 8), cy), :] = scaled
        return carry

    lax.fori_loop(0, cx // UNROLL, scale, 0)

    def sweep(vsrc, vdst, ysrc, ydst):
        def layers(it, carry):
            done = []
            for u in range(UNROLL):
                ix = it * UNROLL + u
                at = pl.multiple_of((ix + 1) * step + EDGE, 8)
                ct = pl.multiple_of((ix + 2) * step + EDGE, 8)
                to = pl.multiple_of(ix * cy, 8)
                center = cpad[pl.ds(ct, cy), :]
                up = wz[pl.ds(to, cy), :][None]
                mid = ysrc[:, pl.ds(at, cy), :]
                total = up * pltpu.roll(mid, LANES - 1, 2) + pltpu.roll(up * mid, 1, 2)
                for d in (step, -step, 1, -1):
                    weight = center + cpad[pl.ds(ct + d, cy), :]
                    total = total + weight[None] * ysrc[:, pl.ds(at + d, cy), :]
                new = vol[:, pl.ds(to, cy), :]
                if vsrc is None:
                    new = (2.0 - OMEGA) * new + total
                else:
                    new = new + (1.0 - OMEGA) * vsrc[:, pl.ds(to, cy), :] + total
                done.append((at, to, new))
            for at, to, new in done:
                vdst[:, pl.ds(to, cy), :] = new
                if ydst is not None:
                    ydst[:, pl.ds(at, cy), :] = new * rd[pl.ds(to, cy), :][None]
                else:
                    lane = lax.broadcasted_iota(jnp.int32, (cy, LANES), 1)
                    out = jnp.where(lane == 1, pltpu.roll(new[1], 1, 1), new[0])
                    out = jnp.where(lane == 2, pltpu.roll(new[2], 2, 1), out)
                    inv = rd[pl.ds(to, cy), :][:, 0:1] * OMEGA
                    xcol[pl.ds(to, cy), :] = out * inv
            return carry

        lax.fori_loop(0, cx // UNROLL, layers, 0)

    def line(kind, j, height):
        if kind == 0:
            base = (j + height) * step + EDGE
            return lambda d: pl.ds(base + d, cy)
        base = height * step + EDGE + j
        return lambda d: pl.ds(base + d, cx, stride=step)

    def flat_line(kind, j):
        return pl.ds(j * cy, cy) if kind == 0 else pl.ds(j, cx, stride=cy)

    def scale_line(kind, j):
        c, flat, yl = line(kind, j, 2), flat_line(kind, j), line(kind, j, 1)
        inv, _ = inverse(cpad[c(0), :], [cpad[c(d), :] for d in (-step, step, -1, 1)])
        rd[flat, :] = inv
        for k in range(3):
            y0[k, yl(0), :] = vol[k, flat, :] * inv

    def sweep_line(kind, j, side=None):
        c, flat, yl = line(kind, j, 2), flat_line(kind, j), line(kind, j, 1)
        center, up, inv = cpad[c(0), :], wz[flat, :], rd[flat, :]
        weights = [(d, center + cpad[c(d), :]) for d in (step, -step, 1, -1)]
        done = []
        for k in range(3):
            mid, first = y0[k, yl(0), :], vol[k, flat, :]
            total = up * pltpu.roll(mid, LANES - 1, 1) + pltpu.roll(up * mid, 1, 1)
            for d, weight in weights:
                total = total + weight * y0[k, yl(d), :]
            done.append((2.0 - OMEGA) * first + total)
        for k in range(3):
            field[k, flat, :] = done[k]
            y1[k, yl(0), :] = done[k] * inv
            if side is not None:
                send_y[0, side, k] = done[k] * inv
        if side is not None:
            send_face(1, side)

    def send_face(turn, side):
        @pl.when(sides[side][0])
        def _():
            face_copy(turn, side, send_y.at[turn - 1, side], recv23.at[turn - 1]).start()

    def take_face(turn, side):
        @pl.when(sides[side][0])
        def _():
            face_wait(turn, side, send_y.at[turn - 1, side], recv23.at[turn - 1]).wait_recv()

    ends = ((0, 0), (0, cx - 1), (1, 0), (1, cy - 1))
    beside = ((0, 1), (0, cx - 2), (1, 1), (1, cy - 2))

    def add_values(turn, dst):
        for side in range(4):
            flat = flat_line(*ends[side])
            for k in range(3):
                dst[k, flat, :] = dst[k, flat, :] + face_w[side] * recv23[turn - 1, side, k]

    sweep(None, field, y0, y1)
    for side in range(4):
        @pl.when(sides[side][0])
        def _(side=side):
            face_wait(0, side, send1.at[side], recv1).wait_recv()
    for index in range(4):
        @pl.when(corners[index][0])
        def _(index=index):
            corner_wait(index).wait_recv()
    half = OMEGA / 2
    for deep in range(2):
        low, high = (1 - deep) * step + EDGE, (cx + 2 + deep) * step + EDGE
        cpad[low:low + cy, :] = recv1[0, 3 + deep] * half
        cpad[high:high + cy, :] = recv1[1, 3 + deep] * half
        cpad[pl.ds(2 * step + EDGE - 1 - deep, cx, stride=step), :] = recv1[2, 3 + deep] * half
        cpad[pl.ds(2 * step + EDGE + cy + deep, cx, stride=step), :] = recv1[3, 3 + deep] * half
    for index in range(4):
        row = (1 + (index // 2) * (cx + 1)) * step + EDGE - 1 + (index % 2) * (cy + 1)
        cpad[row:row + 1, :] = crecv[index, 0:1] * half

    for kind, j in ends:
        scale_line(kind, j)
    for side in range(4):
        if side < 2:
            at = (1 + side * (cx + 1)) * step + EDGE
            inv, _ = inverse(
                cpad[at:at + cy, :],
                [cpad[at + d:at + d + cy, :] for d in (-step, step, -1, 1)],
            )
            for k in range(3):
                y0[k, at - step:at - step + cy, :] = recv1[side, k] * inv
        else:
            at = 2 * step + EDGE - 1 + (side - 2) * (cy + 1)
            inv, _ = inverse(
                cpad[pl.ds(at, cx, stride=step), :],
                [cpad[pl.ds(at + d, cx, stride=step), :] for d in (-step, step, -1, 1)],
            )
            for k in range(3):
                y0[k, pl.ds(at - step, cx, stride=step), :] = recv1[side, k] * inv

    for side in (2, 3, 0, 1):
        sweep_line(*ends[side], side)
    for kind, j in beside:
        sweep_line(kind, j)
    for side, out in enumerate((-step, step, -1, 1)):
        at = line(*ends[side], 2)
        weight = cpad[at(0), :] + cpad[at(out), :]
        face_w[side] = weight
        face_i[side] = weight * rd[flat_line(*ends[side]), :]
    sweep(field, val, y1, y2)
    face = lax.broadcasted_iota(jnp.int32, (1, LANES), 1)
    part = lax.rem(face, cy)
    where = jnp.where(face < cy, part, last + part)
    where = jnp.where(face >= 2 * cy, part * cy, where)
    where = jnp.where(face >= 3 * cy, part * cy + cy - 1, where)
    pick = (lax.broadcasted_iota(jnp.int32, (rows, LANES), 0) == where).astype(f32).astype(bf16)
    hot_face[...] = jnp.dot(hot_ref[...].astype(bf16), pick, preferred_element_type=f32)
    slot_face[...] = jnp.dot(slot_ref[...], pick, preferred_element_type=f32).astype(bf16)

    load_rows[1].wait()
    load_rows[2].wait()
    hot16 = hot_ref[...].astype(bf16)
    slots = slot_ref[...]
    stack = []
    for q in range(2):
        stack += split(param_ref[q:q + 1, :], 2)
    for q in range(2):
        stack.append(span_ref[q:q + 1, :].astype(f32).astype(bf16))
    out = nt_dot(jnp.concatenate([hot16 * part for part in stack], axis=0), slots)
    out = [out[i * n:(i + 1) * n] for i in range(6)]
    meta_send[:, 0, :] = out[0] + out[1]
    meta_send[:, 1, :] = out[2] + out[3]
    meta_send[:, 2, :] = out[4]
    meta_send[:, 3, :] = out[5]
    send_all(*meta)

    for side in (0, 1, 2, 3):
        take_face(1, side)
        at = line(*ends[side], 1)(0)
        for k in range(3):
            new = y2[k, at, :] + face_i[side] * recv23[0, side, k]
            y2[k, at, :] = new
            if side > 1:
                send_y[1, side, k] = new
        if side > 1:
            send_face(2, side)
    for side in (0, 1):
        at = line(*ends[side], 1)(0)
        for k in range(3):
            send_y[1, side, k] = y2[k, at, :]
        send_face(2, side)
    add_values(1, val)
    sweep(val, field, y2, None)


    surf_rows = jnp.concatenate(
        [xcol[c * LANES:(c + 1) * LANES, :].T[0:8] for c in range(rows // LANES)], axis=1
    )
    def route(values, hot16, slots):
        stack = []
        for k in range(3):
            stack += split(values[k:k + 1, :], 2)
        out = nt_dot(jnp.concatenate([hot16 * part for part in stack], axis=0), slots)
        return [out[2 * k * n:(2 * k + 1) * n] + out[(2 * k + 1) * n:(2 * k + 2) * n] for k in range(3)]

    most = route(surf_rows, hot_ref[...].astype(bf16), slot_ref[...])
    for k in range(3):
        surf_send[:, k, :] = most[k]
    surf_send[:, 3, :] = jnp.zeros((n, LANES), f32)

    lane = lax.broadcasted_iota(jnp.int32, (cy, LANES), 1)
    for side in range(4):
        take_face(2, side)
        weight = face_i[side] * OMEGA
        out = jnp.where(lane == 0, weight * recv23[1, side, 0], 0.0)
        for k in (1, 2):
            out = jnp.where(lane == k, pltpu.roll(weight * recv23[1, side, k], k, 1), out)
        xcol[side * cy:(side + 1) * cy, :] = out
    more = route(xcol[0:LANES, :].T[0:8], hot_face[...].astype(bf16), slot_face[...])
    for k in range(3):
        surf_send[:, k, :] = surf_send[:, k, :] + more[k]
    send_all(*surf)
    add_values(2, field)

    every(*meta).wait_recv()
    basis_u = pieces(meta_recv[:, 0, :])
    basis_v = pieces(meta_recv[:, 1, :])
    span_u = meta_recv[:, 2, :].astype(jnp.int32)
    span_v = meta_recv[:, 3, :].astype(jnp.int32)
    knot = lax.broadcasted_iota(jnp.int32, (NC, LANES), 0)

    def spline(span, basis, d):
        offset = knot - span[d:d + 1, :]
        out = jnp.where(offset == 0, basis[0][d:d + 1, :], 0.0)
        for index in range(1, 4):
            out = jnp.where(offset == index, basis[index][d:d + 1, :], out)
        return out

    for d in range(n):
        lanes = slice(d * LANES, (d + 1) * LANES)
        bu_ref[:, lanes] = spline(span_u, basis_u, d)
        high, low = split(spline(span_v, basis_v, d), 2)
        bv_ref[:NC, lanes] = high
        bv_ref[NC:, lanes] = low


    for side in range(4):
        @pl.when(sides[side][0])
        def _(side=side):
            face_copy(0, side, send1.at[side], recv1).wait_send()
            for turn in (1, 2):
                face_copy(turn, side, send_y.at[turn - 1, side], recv23.at[turn - 1]).wait_send()
    for index in range(4):
        @pl.when(corners[index][0])
        def _(index=index):
            corner_copy(index).wait_send()
    every(*meta).wait_send()
    every(*surf).wait_recv()
    every(*surf).wait_send()


def product(n, val, surf_ref, bu_ref, bv_ref, field, grad_ref, sem):
    store = pltpu.make_async_copy(val, field, sem)
    store.start()
    group = 8
    total = jnp.zeros((6 * NC, 2 * NC), jnp.float32)
    for first in range(0, n, group):
        lanes = slice(first * LANES, (first + group) * LANES)
        bu = bu_ref[:, lanes]
        left = jnp.concatenate(
            [
                bu * jnp.concatenate(
                    [surf_ref[d, k:k + 1, :] for d in range(first, first + group)],
                    axis=1,
                )
                for k in range(3)
            ],
            axis=0,
        )
        total = total + nt_dot(jnp.concatenate(split(left, 2), axis=0), bv_ref[:, lanes])
    for k in range(3):
        high, low = total[k * NC:(k + 1) * NC], total[(3 + k) * NC:(4 + k) * NC]
        grad_ref[k] = high[:, :NC] + high[:, NC:] + low[:, :NC] + low[:, NC:]
    store.wait()


def body(volume_sens, stiffness, patch_of_row, knot_spans, span_params):
    ngx, ngy = lax.axis_size("gx"), lax.axis_size("gy")
    n = ngx * ngy
    _, cx, cy, nz = volume_sens.shape
    rows = cx * cy
    step = cy + 2 * EDGE
    f32, bf16 = jnp.float32, jnp.bfloat16
    dma = pltpu.SemaphoreType.DMA
    vmem = pl.BlockSpec(memory_space=pltpu.VMEM)
    room = 62 * 2**20 - 4 * (3 * rows * nz + n * 4 * LANES + 2 * NC * n * LANES)
    found = pl.pallas_call(
        functools.partial(kernel, (ngx, ngy, cx, cy, rows)),
        out_shape=(
            pltpu.VMEM((3, rows, nz), f32),
            pltpu.VMEM((n, 4, LANES), f32),
            pltpu.VMEM((NC, n * LANES), f32),
            pltpu.VMEM((2 * NC, n * LANES), bf16),
        ),
        in_specs=[
            pl.BlockSpec(memory_space=pl.ANY),
            pl.BlockSpec(memory_space=pl.ANY),
            pl.BlockSpec(memory_space=pl.ANY),
            pl.BlockSpec(memory_space=pl.ANY),
            pl.BlockSpec(memory_space=pl.ANY),
        ],
        out_specs=(vmem,) * 4,
        scratch_shapes=[
            pltpu.VMEM((3, rows, nz), f32),
            pltpu.VMEM((rows, nz), f32),
            pltpu.VMEM(((cx + 4) * step, nz), f32),
            pltpu.VMEM((rows, nz), f32),
            pltpu.VMEM((rows, nz), f32),
            pltpu.VMEM((3, rows, nz), f32),
            pltpu.VMEM((3, (cx + 2) * step, nz), f32),
            pltpu.VMEM((3, (cx + 2) * step, nz), f32),
            pltpu.VMEM((3, (cx + 2) * step, nz), f32),
            pltpu.VMEM((4, 5, cy, nz), f32),
            pltpu.VMEM((4, 5, cy, nz), f32),
            pltpu.VMEM((4, 8, nz), f32),
            pltpu.VMEM((4, 8, nz), f32),
            pltpu.VMEM((2, 4, 3, cy, nz), f32),
            pltpu.VMEM((2, 4, 3, cy, nz), f32),
            pltpu.VMEM((n, rows), f32),
            pltpu.VMEM((LANES, rows), bf16),
            pltpu.VMEM((rows, nz), f32),
            pltpu.VMEM((4, cy, nz), f32),
            pltpu.VMEM((4, cy, nz), f32),
            pltpu.VMEM((n, LANES), f32),
            pltpu.VMEM((LANES, LANES), bf16),
            pltpu.VMEM((1, rows), jnp.int32),
            pltpu.VMEM((2, rows), jnp.int32),
            pltpu.VMEM((2, rows), f32),
            pltpu.VMEM((n, 4, LANES), f32),
            pltpu.VMEM((n, 4, LANES), f32),
            pltpu.VMEM((n, 4, LANES), f32),
            dma((7,)),
            dma((12,)),
            dma((12,)),
            dma((4,)),
            dma((4,)),
            dma,
            dma,
            dma,
            dma,
        ],
        compiler_params=pltpu.CompilerParams(
            collective_id=0, has_side_effects=True, vmem_limit_bytes=room
        ),
    )(
        volume_sens.reshape(3, rows, nz),
        stiffness.reshape(rows, nz),
        patch_of_row.reshape(1, rows),
        knot_spans[0].T,
        span_params[0].T,
    )
    field, grads = pl.pallas_call(
        functools.partial(product, n),
        out_shape=(
            jax.ShapeDtypeStruct((3, rows, nz), f32),
            jax.ShapeDtypeStruct((3, NC, NC), f32),
        ),
        in_specs=[vmem] * 4,
        out_specs=(pl.BlockSpec(memory_space=pl.ANY), vmem),
        scratch_shapes=[dma],
        compiler_params=pltpu.CompilerParams(vmem_limit_bytes=32 * 2**20),
    )(*found)
    return field.reshape(volume_sens.shape), grads[None]


def solution(mesh):
    placed = (
        P(None, "gx", "gy", None),
        P("gx", "gy", None),
        P(("gx", "gy"), None, None),
        P(("gx", "gy"), None, None),
        P(("gx", "gy"), None, None),
    )
    return jax.shard_map(
        body,
        mesh=mesh,
        in_specs=placed,
        out_specs=(P(None, "gx", "gy", None), P(("gx", "gy"), None, None, None)),
        check_vma=False,
    )
```
